32 devices in a mesh: groups: 2 (over x), grid: 16 (over z, y, core).
Axes of the slice: x: 2, y: 2, z: 4, core: 2. Of those that a mesh axis runs over, the one named last changes fastest.
Arguments:
- density: bfloat16 [192, 256, 1792], P(('groups', 'grid')), parts along dimension 0, may hold values from -2.5 to 2.5
- block_mask: int32 [192, 7], P(('groups', 'grid')), parts along dimension 0, may hold values 0 or 1
Outputs:
- square: bfloat16 [192, 256, 1792], P(('groups', 'grid')), parts along dimension 0
The draws below stay inside these ranges and needn't reach their ends.
There are 2 independent parts, one for each index of `groups`. The reference program is written for one: setup_inputs(seed, part) draws one part's arguments, and reference() takes and returns one part's arrays. A program takes and returns all parts, laid end to end along the dimension named above; each array names one. Nothing has to cross between parts.
All inputs are finite; a program needn't handle non-finite values. No bound on the sum of `block_mask` on one device may be relied on, other than what follows from the above.
Results may differ from the reference program's by a relative error of at most 0.001.
Values may be sent and summed in bfloat16 or wider, within the bound.
No kernel may reach another device: no remote copies, remote signals or barrier semaphores. Data moves between devices by JAX's collectives and lax.ppermute only.
A program may use at most 64 MiB of HBM per device.

```python
import jax
import jax.numpy as jnp

B = 256
REACH = 3
BAND = 7
NBLK = 96


def touch_ends(values, own_key, smallest, top_value):
    extent = values.shape
    place = [jax.random.randint(jax.random.fold_in(own_key, axis), (), 0, extent[axis]) for axis in range(len(extent))]
    values = values.at[tuple(place)].set(smallest)
    longest = extent.index(max(extent))
    place[longest] = (place[longest] + 1) % extent[longest]
    return values.at[tuple(place)].set(top_value)


def block_levels(stream_key, shape, shards, least, largest):
    def one(position, blocks):
        draws = jax.random.uniform(jax.random.fold_in(jax.random.fold_in(stream_key, 6), position), (blocks,), jnp.float32, least / len(shards), largest / len(shards))
        return jnp.repeat(jnp.exp(draws), shape[position] // blocks).reshape((-1,) + (1,) * (len(shape) - position - 1))

    gain = one(*shards[0])
    for cut in shards[1:]:
        gain = gain * one(*cut)
    return gain


def bell_draw(rng, dims, scale, most, pieces=(), kind=jnp.bfloat16):
    array = jax.random.normal(rng, dims, jnp.float32) * scale
    if len(pieces) > 0:
        array = block_levels(rng, dims, pieces, -0.22, 0.18) * array
    return jnp.clip(array, min=-most, max=most).astype(kind)


def setup_inputs(seed: int = 0, part: int = 0) -> dict:
    keys = jax.random.split(jax.random.key(seed), 3)
    own_keys = jax.random.split(jax.random.fold_in(keys[2], part), 3)
    density = bell_draw(own_keys[0], (NBLK, B, BAND * B), 0.17, 2.5, ((0, 16),))
    block_mask = touch_ends((jax.random.randint(own_keys[1], (NBLK, BAND), 0, 8) < 7).astype(jnp.int32), jax.random.fold_in(own_keys[1], 1), 0, 1)
    return {"density": density, "block_mask": block_mask}


def reference(density, block_mask):
    width = B
    reach = REACH
    nrows = density.shape[0]
    expand = jnp.repeat(block_mask.astype(density.dtype), width, axis=1)
    masked = density * expand[:, None, :]
    extended = jnp.concatenate([masked[nrows - reach:], masked, masked[:reach]], axis=0)
    totals = jnp.zeros((nrows, width, BAND * width), jnp.float32)
    for first in range(-reach, reach + 1):
        low = max(-reach, -reach - first)
        high = min(reach, reach - first)
        left = masked[:, :, (first + reach) * width:(first + reach + 1) * width].astype(jnp.float32)
        right = extended[reach + first:reach + first + nrows, :, (low + reach) * width:(high + reach + 1) * width].astype(jnp.float32)
        part = jnp.einsum('nab,nbc->nac', left, right)
        start = (first + low + reach) * width
        totals = totals.at[:, :, start:start + part.shape[2]].add(part)
    return (totals * expand[:, None, :].astype(jnp.float32)).astype(jnp.bfloat16)
```

```python
import jax
import jax.numpy as jnp
from jax import lax
from jax.experimental import pallas as pl
from jax.experimental.pallas import tpu as pltpu
from jax.sharding import PartitionSpec as P

F32 = jnp.float32
BF16 = jnp.bfloat16
VMEM_BYTES = 56 * 1024 * 1024


class Band:
    def __init__(self, rows, width, band):
        self.rows = rows
        self.width = width
        self.band = band
        self.reach = reach = (band - 1) // 2
        corner = [(k, j) for k in range(-1, -reach - 1, -1) for j in range(0, k + reach + 1)]
        self.first = [b for b in corner if b[0] > -reach]
        self.second = [b for b in corner if b[0] == -reach] + [(k, -1) for k in range(-1, -reach - 1, -1)]
        self.third = [(k, j) for j in range(-2, -reach - 1, -1) for k in range(-1, -reach - 1, -1)]
        touched = [(i, j) for i in range(reach) for j in range(i - reach, reach)]
        self.last_targets = [t for t in touched if t[1] < -1]
        self.second_targets = [t for t in touched if t[1] == -1 or t == (0, 0)]
        self.first_targets = [t for t in touched if t[1] >= 0 and t != (0, 0)]

    def at(self, side, x):
        return x if side == 0 else self.rows - 1 - x

    def slot(self, side, i, j):
        return (j - i if side == 0 else i - j) + self.reach

    def cols(self, slot, count=1):
        return pl.ds(slot * self.width, count * self.width)

    def sent(self, side, block):
        k, j = block
        return (k + self.rows if side == 0 else -1 - k), self.slot(side, k, j)

    def inner(self, i, j, low, high):
        return [k for k in range(max(low, i - self.reach, j - self.reach), min(high, i + self.reach, j + self.reach) + 1)]


def dot(a, b):
    return jnp.dot(a, b, preferred_element_type=F32)


def spec(space):
    return pl.BlockSpec(memory_space=space)


def call(kernel, outs, scratch, args, aliases=None, flops=0, name=None):
    moved = sum(a.size * a.dtype.itemsize for a in args) + sum(o.size * o.dtype.itemsize for o, _ in outs)
    return pl.pallas_call(
        kernel,
        out_shape=[o for o, _ in outs],
        in_specs=[spec(pltpu.SMEM)] + [spec(pl.ANY)] * (len(args) - 1),
        out_specs=[spec(space) for _, space in outs],
        scratch_shapes=scratch,
        input_output_aliases=aliases or {},
        compiler_params=pltpu.CompilerParams(vmem_limit_bytes=VMEM_BYTES),
        cost_estimate=pl.CostEstimate(flops=flops, bytes_accessed=moved, transcendentals=0),
        name=name,
    )(*args)


def pack(g, blocks, mask, density):
    def kernel(mask_ref, density_ref, *refs):
        outs, sems = refs[:2], refs[2]
        copies = []
        for side in range(2):
            for n, block in enumerate(blocks):
                row, slot = g.sent(side, block)
                copy = pltpu.make_async_copy(
                    density_ref.at[row, :, g.cols(slot)], outs[side].at[n], sems.at[side, n]
                )
                copy.start()
                copies.append((copy, side, n, row, slot))
        for copy, side, n, row, slot in copies:
            copy.wait()

            @pl.when(mask_ref[row, slot] == 0)
            def _():
                outs[side][n] = jnp.zeros((g.width, g.width), BF16)

    out = jax.ShapeDtypeStruct((len(blocks), g.width, g.width), BF16)
    return call(
        kernel,
        [(out, pltpu.VMEM)] * 2,
        [pltpu.SemaphoreType.DMA((2, len(blocks)))],
        (mask, density),
        name="pack",
    )


def local(g, mask, density):
    rows, width, strip = density.shape
    reach, band = g.reach, g.band

    def kernel(mask_ref, density_ref, out_ref, sum_ref, own, sums, done, in_sems, out_sems):
        loads = [pltpu.make_async_copy(density_ref.at[r], own.at[r], in_sems.at[r]) for r in range(rows)]
        for load in loads:
            load.start()
        for r in range(rows):
            loads[r].wait()
            for s in range(band):

                @pl.when(mask_ref[r, s] == 0)
                def _():
                    own[r, :, g.cols(s)] = jnp.zeros((width, width), BF16)

        stores = []
        for i in range(rows):
            side = 0 if 2 * i < rows else 1
            near = g.at(side, i)
            final = max(0, band - 2 * reach + near)
            for s in range(band):
                j = i + s - reach
                total = None
                for k in g.inner(i, j, 0, rows - 1):
                    part = dot(own[i, :, g.cols(k - i + reach)], own[k, :, g.cols(j - k + reach)])
                    total = part if total is None else total + part
                ends = s >= band - final if side == 0 else s < final
                if ends:
                    done[i, :, g.cols(s)] = jnp.where(mask_ref[i, s] == 0, 0.0, total).astype(BF16)
                else:
                    sums[i, :, g.cols(s)] = total
            keep = g.cols(0, band - final) if side == 0 else g.cols(final, band - final)
            give = g.cols(band - final, final) if side == 0 else g.cols(0, final)
            stores.append(pltpu.make_async_copy(sums.at[i, :, keep], sum_ref.at[i, :, keep], out_sems.at[0, i]))
            stores.append(pltpu.make_async_copy(done.at[i, :, give], out_ref.at[i, :, give], out_sems.at[1, i]))
            stores[-2].start()
            stores[-1].start()
        for store in stores:
            store.wait()

    return call(
        kernel,
        [
            (jax.ShapeDtypeStruct(density.shape, BF16), pl.ANY),
            (jax.ShapeDtypeStruct(density.shape, F32), pl.ANY),
        ],
        [
            pltpu.VMEM(density.shape, BF16),
            pltpu.VMEM(density.shape, F32),
            pltpu.VMEM(density.shape, BF16),
            pltpu.SemaphoreType.DMA((rows,)),
            pltpu.SemaphoreType.DMA((2, rows)),
        ],
        (mask, density),
        flops=2 * 160 * width**3,
        name="local",
    )


def add_halo(g, targets, lists, mask, density, sums, halos, out, name):
    width, reach = g.width, g.reach
    blocks = [b for part in lists for b in part]
    terms = {(i, j): [k for k in g.inner(i, j, -reach, -1) if (k, j) in blocks] for i, j in targets}
    lefts = sorted({(i, k) for (i, j), ks in terms.items() for k in ks})
    where = {b: (p, n) for p, part in enumerate(lists) for n, b in enumerate(part)}
    nparts = len(lists)
    nt, nl, nb = len(targets), len(lefts), len(blocks)

    def kernel(mask_ref, density_ref, sum_ref, *refs):
        halo_refs = refs[: 2 * nparts]
        out_ref = refs[2 * nparts + 1]
        right, left, total, done, in_sems, out_sems = refs[2 * nparts + 2 :]
        waits = []
        for side in range(2):
            base = 0
            for p, part in enumerate(lists):
                waits.append(
                    pltpu.make_async_copy(
                        halo_refs[2 * p + side], right.at[side, pl.ds(base, len(part))], in_sems.at[side, p]
                    )
                )
                base += len(part)
            for n, (i, k) in enumerate(lefts):
                source = density_ref.at[g.at(side, i), :, g.cols(g.slot(side, i, k))]
                waits.append(pltpu.make_async_copy(source, left.at[side, n], in_sems.at[side, nparts + n]))
            for n, (i, j) in enumerate(targets):
                source = sum_ref.at[g.at(side, i), :, g.cols(g.slot(side, i, j))]
                waits.append(pltpu.make_async_copy(source, total.at[side, n], in_sems.at[side, nparts + nl + n]))
        for copy in waits:
            copy.start()
        for copy in waits:
            copy.wait()
        for side in range(2):
            for n, (i, k) in enumerate(lefts):

                @pl.when(mask_ref[g.at(side, i), g.slot(side, i, k)] == 0)
                def _():
                    left[side, n] = jnp.zeros((width, width), BF16)

        stores = []
        for side in range(2):
            for n, (i, j) in enumerate(targets):
                value = total[side, n]
                for k in terms[i, j]:
                    p, m = where[k, j]
                    base = sum(len(part) for part in lists[:p])
                    value += dot(left[side, lefts.index((i, k))], right[side, base + m])
                row, slot = g.at(side, i), g.slot(side, i, j)
                done[side, n] = jnp.where(mask_ref[row, slot] == 0, 0.0, value).astype(BF16)
                store = pltpu.make_async_copy(done.at[side, n], out_ref.at[row, :, g.cols(slot)], out_sems.at[side, n])
                store.start()
                stores.append(store)
        for store in stores:
            store.wait()

    block = (width, width)
    return call(
        kernel,
        [(jax.ShapeDtypeStruct(out.shape, out.dtype), pl.ANY)],
        [
            pltpu.VMEM((2, nb) + block, BF16),
            pltpu.VMEM((2, nl) + block, BF16),
            pltpu.VMEM((2, nt) + block, F32),
            pltpu.VMEM((2, nt) + block, BF16),
            pltpu.SemaphoreType.DMA((2, nparts + nl + nt)),
            pltpu.SemaphoreType.DMA((2, nt)),
        ],
        (mask, density, sums, *[h for pair in halos for h in pair], out),
        aliases={3 + 2 * nparts: 0},
        flops=2 * 2 * sum(len(ks) for ks in terms.values()) * width**3,
        name=name,
    )[0]


def on_device(density, block_mask):
    rows, width, strip = density.shape
    g = Band(rows, width, block_mask.shape[1])
    count = lax.axis_size("grid")
    up = [(i, (i + 1) % count) for i in range(count)]
    down = [((i + 1) % count, i) for i in range(count)]

    def swap(pair):
        return lax.ppermute(pair[0], "grid", up), lax.ppermute(pair[1], "grid", down)

    first = swap(pack(g, g.first, block_mask, density))
    second = swap(pack(g, g.second, block_mask, density))
    third = swap(pack(g, g.third, block_mask, density))
    out, sums = local(g, block_mask, density)
    out = add_halo(g, g.first_targets, [g.first], block_mask, density, sums, [first], out, "corner")
    out = add_halo(g, g.second_targets, [g.first, g.second], block_mask, density, sums, [first, second], out, "edge")
    return add_halo(g, g.last_targets, [g.third], block_mask, density, sums, [third], out, "last")


def solution(mesh):
    in_specs = (P(("groups", "grid"), None, None), P(("groups", "grid"), None))
    out_specs = P(("groups", "grid"), None, None)
    return jax.shard_map(on_device, mesh=mesh, in_specs=in_specs, out_specs=out_specs, check_vma=False)
```

```python
import jax
import jax.numpy as jnp
from jax import lax
from jax.experimental import pallas as pl
from jax.experimental.pallas import tpu as pltpu
from jax.sharding import PartitionSpec as P

F32 = jnp.float32
BF16 = jnp.bfloat16
VMEM_BYTES = 26 * 1024 * 1024


class Band:
    def __init__(self, rows, width, band):
        self.rows = rows
        self.width = width
        self.band = band
        self.reach = reach = (band - 1) // 2
        corner = [(k, j) for k in range(-1, -reach - 1, -1) for j in range(0, k + reach + 1)]
        self.first = [b for b in corner if b[0] > -reach]
        self.second = [b for b in corner if b[0] == -reach] + [(k, -1) for k in range(-1, -reach - 1, -1)]
        touched = [(i, j) for i in range(reach) for j in range(i - reach, reach)]
        self.last_targets = [t for t in touched if t[1] < -1]
        self.second_targets = [t for t in touched if t[1] == -1 or t == (0, 0)]
        self.first_targets = [t for t in touched if t[1] >= 0 and t != (0, 0)]

    def at(self, side, x):
        return x if side == 0 else self.rows - 1 - x

    def slot(self, side, i, j):
        return (j - i if side == 0 else i - j) + self.reach

    def cols(self, slot, count=1):
        return pl.ds(slot * self.width, count * self.width)

    def sent(self, side, block):
        k, j = block
        return (k + self.rows if side == 0 else -1 - k), self.slot(side, k, j)

    def inner(self, i, j, low, high):
        return [k for k in range(max(low, i - self.reach, j - self.reach), min(high, i + self.reach, j + self.reach) + 1)]


def dot(a, b):
    return jnp.dot(a, b, preferred_element_type=F32)


def spec(space):
    return pl.BlockSpec(memory_space=space)


def call(kernel, ins, outs, scratch, args, aliases=None, flops=0, name=None):
    moved = sum(a.size * a.dtype.itemsize for a in args) + sum(o.size * o.dtype.itemsize for o, _ in outs)
    return pl.pallas_call(
        kernel,
        out_shape=[o for o, _ in outs],
        in_specs=[spec(space) for space in ins],
        out_specs=[spec(space) for _, space in outs],
        scratch_shapes=scratch,
        input_output_aliases=aliases or {},
        compiler_params=pltpu.CompilerParams(vmem_limit_bytes=VMEM_BYTES),
        cost_estimate=pl.CostEstimate(flops=flops, bytes_accessed=moved, transcendentals=0),
        name=name,
    )(*args)


def pack(g, blocks, mask, density):
    def kernel(mask_ref, density_ref, *refs):
        outs, sems = refs[:2], refs[2]
        copies = []
        for side in range(2):
            for n, block in enumerate(blocks):
                row, slot = g.sent(side, block)
                copy = pltpu.make_async_copy(
                    density_ref.at[row, :, g.cols(slot)], outs[side].at[n], sems.at[side, n]
                )
                copy.start()
                copies.append((copy, side, n, row, slot))
        for copy, side, n, row, slot in copies:
            copy.wait()

            @pl.when(mask_ref[row, slot] == 0)
            def _():
                outs[side][n] = jnp.zeros((g.width, g.width), BF16)

    out = jax.ShapeDtypeStruct((len(blocks), g.width, g.width), BF16)
    return call(
        kernel,
        [pltpu.SMEM, pltpu.HBM],
        [(out, pltpu.VMEM)] * 2,
        [pltpu.SemaphoreType.DMA((2, len(blocks)))],
        (mask, density),
        name="pack",
    )


def local(g, mask, density):
    rows, width, strip = density.shape
    reach, band = g.reach, g.band

    def kernel(mask_ref, density_ref, out_ref, own, sums, done, in_sems, out_sems):
        loads = [pltpu.make_async_copy(density_ref.at[r], own.at[r], in_sems.at[r]) for r in range(rows)]
        for load in loads:
            load.start()
        for r in range(rows):
            loads[r].wait()
            for s in range(band):

                @pl.when(mask_ref[r, s] == 0)
                def _():
                    own[r, :, g.cols(s)] = jnp.zeros((width, width), BF16)

        stores = []
        for i in range(rows):
            side = 0 if 2 * i < rows else 1
            final = max(0, band - 2 * reach + g.at(side, i))
            for s in range(band):
                j = i + s - reach
                total = None
                for k in g.inner(i, j, 0, rows - 1):
                    part = dot(own[i, :, g.cols(k - i + reach)], own[k, :, g.cols(j - k + reach)])
                    total = part if total is None else total + part
                ends = s >= band - final if side == 0 else s < final
                if ends:
                    done[i, :, g.cols(s)] = jnp.where(mask_ref[i, s] == 0, 0.0, total).astype(BF16)
                else:
                    sums[i, :, g.cols(s)] = total
            give = g.cols(band - final, final) if side == 0 else g.cols(0, final)
            stores.append(pltpu.make_async_copy(done.at[i, :, give], out_ref.at[i, :, give], out_sems.at[i]))
            stores[-1].start()
        for store in stores:
            store.wait()

    return call(
        kernel,
        [pltpu.SMEM, pltpu.HBM],
        [
            (jax.ShapeDtypeStruct(density.shape, BF16), pltpu.HBM),
            (jax.ShapeDtypeStruct(density.shape, BF16), pltpu.VMEM),
            (jax.ShapeDtypeStruct(density.shape, F32), pltpu.VMEM),
        ],
        [
            pltpu.VMEM(density.shape, BF16),
            pltpu.SemaphoreType.DMA((rows,)),
            pltpu.SemaphoreType.DMA((rows,)),
        ],
        (mask, density),
        flops=2 * 160 * width**3,
        name="local",
    )


CODE_BITS = 15
CODE_ROWS = 16


def partials(g, own, first):
    width, reach, rows = g.width, g.reach, g.rows
    targets = g.last_targets

    def kernel(own_ref, above_ref, below_ref, *outs):
        halos = (above_ref, below_ref)
        for side in range(2):
            row_ids = lax.broadcasted_iota(jnp.int32, (CODE_ROWS, width), 0)
            powers = jnp.zeros((CODE_ROWS, width), F32)
            for n, (i, j) in enumerate(targets):
                total = None
                for k in g.inner(i, j, -reach, -1):
                    left = halos[1 - side][g.first.index((-1 - i, -1 - k))]
                    row, slot = g.sent(side, (k, j))
                    part = dot(left, own_ref[row, :, g.cols(slot)])
                    total = part if total is None else total + part
                top = jnp.maximum(jnp.max(jnp.abs(total), axis=0, keepdims=True), 2.0**-100)
                power = jnp.ceil(jnp.log2(top) + 0.001)
                code = jnp.round(total * jnp.exp2(CODE_BITS - power))
                outs[side][pl.ds(n * width, width), :] = code.astype(jnp.int32).astype(jnp.int16)
                powers = jnp.where(row_ids == n, power, powers)
            outs[side][pl.ds(len(targets) * width, CODE_ROWS), :] = powers.astype(jnp.int32).astype(jnp.int16)

    out = jax.ShapeDtypeStruct((len(targets) * width + CODE_ROWS, width), jnp.int16)
    return call(
        kernel,
        [pltpu.VMEM] * 3,
        [(out, pltpu.VMEM)] * 2,
        [],
        (own, *first),
        flops=2 * 2 * 8 * width**3,
        name="partials",
    )


def finish(g, targets, mask, sums, out, term_of, operands, flops, name):
    width = g.width
    nt, nops = len(targets), len(operands)

    def kernel(mask_ref, sum_ref, *refs):
        ins, (out_ref, done, sems) = refs[:nops], refs[nops + 1 :]
        stores = []
        for side in range(2):
            for n, (i, j) in enumerate(targets):
                row, slot = g.at(side, i), g.slot(side, i, j)
                value = sum_ref[row, :, g.cols(slot)] + term_of(ins, side, i, j)
                done[side, n] = jnp.where(mask_ref[row, slot] == 0, 0.0, value).astype(BF16)
                store = pltpu.make_async_copy(done.at[side, n], out_ref.at[row, :, g.cols(slot)], sems.at[side, n])
                store.start()
                stores.append(store)
        for store in stores:
            store.wait()

    return call(
        kernel,
        [pltpu.SMEM] + [pltpu.VMEM] * (1 + nops) + [pltpu.HBM],
        [(jax.ShapeDtypeStruct(out.shape, out.dtype), pltpu.HBM)],
        [
            pltpu.VMEM((2, nt, width, width), BF16),
            pltpu.SemaphoreType.DMA((2, nt)),
        ],
        (mask, sums, *operands, out),
        aliases={2 + nops: 0},
        flops=flops,
        name=name,
    )[0]


def with_halo(g, targets, lists, mask, own, sums, halos, out, name):
    where = {b: (p, n) for p, part in enumerate(lists) for n, b in enumerate(part)}

    def inner(i, j):
        return [k for k in g.inner(i, j, -g.reach, -1) if (k, j) in where]

    def term_of(ins, side, i, j):
        total = None
        for k in inner(i, j):
            p, n = where[k, j]
            part = dot(ins[0][g.at(side, i), :, g.cols(g.slot(side, i, k))], ins[1 + 2 * p + side][n])
            total = part if total is None else total + part
        return total

    operands = (own, *[h for pair in halos for h in pair])
    flops = 2 * 2 * sum(len(inner(i, j)) for i, j in targets) * g.width**3
    return finish(g, targets, mask, sums, out, term_of, operands, flops, name)


def with_partials(g, mask, sums, coded, out):
    width, targets = g.width, g.last_targets

    def term_of(ins, side, i, j):
        n = targets.index((i, j))
        code = ins[side][pl.ds(n * width, width), :].astype(jnp.int32).astype(F32)
        power = ins[side][pl.ds(len(targets) * width, CODE_ROWS), :].astype(jnp.int32).astype(F32)[n : n + 1]
        return code * jnp.exp2(power - CODE_BITS)

    return finish(g, targets, mask, sums, out, term_of, coded, 0, "last")


def on_device(density, block_mask):
    rows, width, strip = density.shape
    g = Band(rows, width, block_mask.shape[1])
    count = lax.axis_size("grid")
    up = [(i, (i + 1) % count) for i in range(count)]
    down = [((i + 1) % count, i) for i in range(count)]

    def swap(pair):
        return lax.ppermute(pair[0], "grid", up), lax.ppermute(pair[1], "grid", down)

    first = swap(pack(g, g.first, block_mask, density))
    second = swap(pack(g, g.second, block_mask, density))
    out, own, sums = local(g, block_mask, density)
    coded = swap(partials(g, own, first))
    out = with_halo(g, g.first_targets, [g.first], block_mask, own, sums, [first], out, "corner")
    out = with_halo(g, g.second_targets, [g.first, g.second], block_mask, own, sums, [first, second], out, "edge")
    return with_partials(g, block_mask, sums, coded, out)


def solution(mesh):
    in_specs = (P(("groups", "grid"), None, None), P(("groups", "grid"), None))
    out_specs = P(("groups", "grid"), None, None)
    return jax.shard_map(on_device, mesh=mesh, in_specs=in_specs, out_specs=out_specs, check_vma=False)
```

```python
import jax
import jax.numpy as jnp
from jax import lax
from jax.experimental import pallas as pl
from jax.experimental.pallas import tpu as pltpu
from jax.sharding import PartitionSpec as P

F32 = jnp.float32
BF16 = jnp.bfloat16
VMEM_BYTES = 26 * 1024 * 1024


class Band:
    def __init__(self, rows, width, band):
        self.rows = rows
        self.width = width
        self.band = band
        self.reach = reach = (band - 1) // 2
        corner = [(k, j) for k in range(-1, -reach - 1, -1) for j in range(0, k + reach + 1)]
        self.first = [b for b in corner if b[0] > -reach]
        self.second = [b for b in corner if b[0] == -reach] + [(k, -1) for k in range(-1, -reach - 1, -1)]
        touched = [(i, j) for i in range(reach) for j in range(i - reach, reach)]
        self.last_targets = [t for t in touched if t[1] < -1]
        self.second_targets = [t for t in touched if t[1] == -1 or t == (0, 0)]
        self.first_targets = [t for t in touched if t[1] >= 0 and t != (0, 0)]

    def at(self, side, x):
        return x if side == 0 else self.rows - 1 - x

    def slot(self, side, i, j):
        return (j - i if side == 0 else i - j) + self.reach

    def cols(self, slot, count=1):
        return pl.ds(slot * self.width, count * self.width)

    def sent(self, side, block):
        k, j = block
        return (k + self.rows if side == 0 else -1 - k), self.slot(side, k, j)

    def inner(self, i, j, low, high):
        return [k for k in range(max(low, i - self.reach, j - self.reach), min(high, i + self.reach, j + self.reach) + 1)]


def dot(a, b):
    return jnp.dot(a, b, preferred_element_type=F32)


def spec(space):
    return pl.BlockSpec(memory_space=space)


def in_hbm(x):
    return pltpu.with_memory_space_constraint(x, pltpu.HBM)


def call(kernel, ins, outs, scratch, args, aliases=None, flops=0, name=None):
    moved = sum(a.size * a.dtype.itemsize for a in args) + sum(o.size * o.dtype.itemsize for o, _ in outs)
    return pl.pallas_call(
        kernel,
        out_shape=[o for o, _ in outs],
        in_specs=[spec(space) for space in ins],
        out_specs=[spec(space) for _, space in outs],
        scratch_shapes=scratch,
        input_output_aliases=aliases or {},
        compiler_params=pltpu.CompilerParams(vmem_limit_bytes=VMEM_BYTES),
        cost_estimate=pl.CostEstimate(flops=flops, bytes_accessed=moved, transcendentals=0),
        name=name,
    )(*args)


def pack(g, blocks, mask, density):
    def kernel(mask_ref, density_ref, *refs):
        outs, (marks, mark_sem, sems) = refs[:2], refs[2:]
        mark = pltpu.make_async_copy(mask_ref, marks, mark_sem)
        mark.start()
        copies = []
        for side in range(2):
            for n, block in enumerate(blocks):
                row, slot = g.sent(side, block)
                copy = pltpu.make_async_copy(
                    density_ref.at[row, :, g.cols(slot)], outs[side].at[n], sems.at[side, n]
                )
                copy.start()
                copies.append((copy, side, n, row, slot))
        mark.wait()
        for copy, side, n, row, slot in copies:
            copy.wait()

            @pl.when(marks[row, slot] == 0)
            def _():
                outs[side][n] = jnp.zeros((g.width, g.width), BF16)

    out = jax.ShapeDtypeStruct((len(blocks), g.width, g.width), BF16)
    return call(
        kernel,
        [pltpu.HBM, pltpu.HBM],
        [(out, pltpu.VMEM)] * 2,
        [
            pltpu.SMEM(mask.shape, jnp.int32),
            pltpu.SemaphoreType.DMA,
            pltpu.SemaphoreType.DMA((2, len(blocks))),
        ],
        (in_hbm(mask), in_hbm(density)),
        name="pack",
    )


def local(g, mask, density):
    rows, width, strip = density.shape
    reach, band = g.reach, g.band

    def kernel(mask_ref, density_ref, out_ref, own, sums, done, in_sems, out_sems):
        loads = [pltpu.make_async_copy(density_ref.at[r], own.at[r], in_sems.at[r]) for r in range(rows)]
        for load in loads:
            load.start()
        for r in range(rows):
            loads[r].wait()
            for s in range(band):

                @pl.when(mask_ref[r, s] == 0)
                def _():
                    own[r, :, g.cols(s)] = jnp.zeros((width, width), BF16)

        stores = []
        for i in range(rows):
            side = 0 if 2 * i < rows else 1
            final = max(0, band - 2 * reach + g.at(side, i))
            for s in range(band):
                j = i + s - reach
                total = None
                for k in g.inner(i, j, 0, rows - 1):
                    part = dot(own[i, :, g.cols(k - i + reach)], own[k, :, g.cols(j - k + reach)])
                    total = part if total is None else total + part
                ends = s >= band - final if side == 0 else s < final
                if ends:
                    done[i, :, g.cols(s)] = jnp.where(mask_ref[i, s] == 0, 0.0, total).astype(BF16)
                else:
                    sums[i, :, g.cols(s)] = total
            give = g.cols(band - final, final) if side == 0 else g.cols(0, final)
            stores.append(pltpu.make_async_copy(done.at[i, :, give], out_ref.at[i, :, give], out_sems.at[i]))
            stores[-1].start()
        for store in stores:
            store.wait()

    return call(
        kernel,
        [pltpu.SMEM, pltpu.HBM],
        [
            (jax.ShapeDtypeStruct(density.shape, BF16), pltpu.HBM),
            (jax.ShapeDtypeStruct(density.shape, BF16), pltpu.VMEM),
            (jax.ShapeDtypeStruct(density.shape, F32), pltpu.VMEM),
        ],
        [
            pltpu.VMEM(density.shape, BF16),
            pltpu.SemaphoreType.DMA((rows,)),
            pltpu.SemaphoreType.DMA((rows,)),
        ],
        (mask, in_hbm(density)),
        flops=2 * 160 * width**3,
        name="local",
    )


CODE_BITS = 15
CODE_ROWS = 16


def partials(g, own, first):
    width, reach, rows = g.width, g.reach, g.rows
    targets = g.last_targets

    def kernel(own_ref, above_ref, below_ref, *outs):
        halos = (above_ref, below_ref)
        for side in range(2):
            row_ids = lax.broadcasted_iota(jnp.int32, (CODE_ROWS, width), 0)
            powers = jnp.zeros((CODE_ROWS, width), F32)
            for n, (i, j) in enumerate(targets):
                total = None
                for k in g.inner(i, j, -reach, -1):
                    left = halos[1 - side][g.first.index((-1 - i, -1 - k))]
                    row, slot = g.sent(side, (k, j))
                    part = dot(left, own_ref[row, :, g.cols(slot)])
                    total = part if total is None else total + part
                top = jnp.maximum(jnp.max(jnp.abs(total), axis=0, keepdims=True), 2.0**-100)
                power = jnp.ceil(jnp.log2(top) + 0.001)
                code = jnp.round(total * jnp.exp2(CODE_BITS - power))
                outs[side][pl.ds(n * width, width), :] = code.astype(jnp.int32).astype(jnp.int16)
                powers = jnp.where(row_ids == n, power, powers)
            outs[side][pl.ds(len(targets) * width, CODE_ROWS), :] = powers.astype(jnp.int32).astype(jnp.int16)

    out = jax.ShapeDtypeStruct((len(targets) * width + CODE_ROWS, width), jnp.int16)
    return call(
        kernel,
        [pltpu.VMEM] * 3,
        [(out, pltpu.VMEM)] * 2,
        [],
        (own, *first),
        flops=2 * 2 * 8 * width**3,
        name="partials",
    )


def finish(g, targets, mask, sums, out, term_of, operands, flops, name):
    width = g.width
    nt, nops = len(targets), len(operands)

    def kernel(mask_ref, sum_ref, *refs):
        ins, (out_ref, done, sems) = refs[:nops], refs[nops + 1 :]
        stores = []
        for side in range(2):
            for n, (i, j) in enumerate(targets):
                row, slot = g.at(side, i), g.slot(side, i, j)
                value = sum_ref[row, :, g.cols(slot)] + term_of(ins, side, i, j)
                done[side, n] = jnp.where(mask_ref[row, slot] == 0, 0.0, value).astype(BF16)
                store = pltpu.make_async_copy(done.at[side, n], out_ref.at[row, :, g.cols(slot)], sems.at[side, n])
                store.start()
                stores.append(store)
        for store in stores:
            store.wait()

    return call(
        kernel,
        [pltpu.SMEM] + [pltpu.VMEM] * (1 + nops) + [pltpu.HBM],
        [(jax.ShapeDtypeStruct(out.shape, out.dtype), pltpu.HBM)],
        [
            pltpu.VMEM((2, nt, width, width), BF16),
            pltpu.SemaphoreType.DMA((2, nt)),
        ],
        (mask, sums, *operands, out),
        aliases={2 + nops: 0},
        flops=flops,
        name=name,
    )[0]


def with_halo(g, targets, lists, mask, own, sums, halos, out, name):
    where = {b: (p, n) for p, part in enumerate(lists) for n, b in enumerate(part)}

    def inner(i, j):
        return [k for k in g.inner(i, j, -g.reach, -1) if (k, j) in where]

    def term_of(ins, side, i, j):
        total = None
        for k in inner(i, j):
            p, n = where[k, j]
            part = dot(ins[0][g.at(side, i), :, g.cols(g.slot(side, i, k))], ins[1 + 2 * p + side][n])
            total = part if total is None else total + part
        return total

    operands = (own, *[h for pair in halos for h in pair])
    flops = 2 * 2 * sum(len(inner(i, j)) for i, j in targets) * g.width**3
    return finish(g, targets, mask, sums, out, term_of, operands, flops, name)


def with_partials(g, mask, sums, coded, out):
    width, targets = g.width, g.last_targets

    def term_of(ins, side, i, j):
        n = targets.index((i, j))
        code = ins[side][pl.ds(n * width, width), :].astype(jnp.int32).astype(F32)
        power = ins[side][pl.ds(len(targets) * width, CODE_ROWS), :].astype(jnp.int32).astype(F32)[n : n + 1]
        return code * jnp.exp2(power - CODE_BITS)

    return finish(g, targets, mask, sums, out, term_of, coded, 0, "last")


def on_device(density, block_mask):
    rows, width, strip = density.shape
    g = Band(rows, width, block_mask.shape[1])
    count = lax.axis_size("grid")
    up = [(i, (i + 1) % count) for i in range(count)]
    down = [((i + 1) % count, i) for i in range(count)]

    def swap(pair):
        return lax.ppermute(pair[0], "grid", up), lax.ppermute(pair[1], "grid", down)

    first = swap(pack(g, g.first, block_mask, density))
    second = swap(pack(g, g.second, block_mask, density))
    out, own, sums = local(g, block_mask, density)
    coded = swap(partials(g, own, first))
    out = with_halo(g, g.first_targets, [g.first], block_mask, own, sums, [first], out, "corner")
    out = with_halo(g, g.second_targets, [g.first, g.second], block_mask, own, sums, [first, second], out, "edge")
    return with_partials(g, block_mask, sums, coded, out)


def solution(mesh):
    in_specs = (P(("groups", "grid"), None, None), P(("groups", "grid"), None))
    out_specs = P(("groups", "grid"), None, None)
    return jax.shard_map(on_device, mesh=mesh, in_specs=in_specs, out_specs=out_specs, check_vma=False)
```

```python
import jax
import jax.numpy as jnp
from jax import lax
from jax.experimental import pallas as pl
from jax.experimental.pallas import tpu as pltpu
from jax.sharding import PartitionSpec as P

F32 = jnp.float32
BF16 = jnp.bfloat16
VMEM_BYTES = 26 * 1024 * 1024
CODE_BITS = 15
WEIGHT = 100
CODE_ROWS = 16
FAR, NEAR = 0, 1


def neighbour_side(link):
    odd = lax.rem(lax.axis_index("grid"), 2)
    return odd if link == FAR else 1 - odd


def exchange(x, link):
    count = lax.axis_size("grid")
    step = [1 if (i % 2 == 0) == (link == NEAR) else -1 for i in range(count)]
    return lax.ppermute(x, "grid", [(i, (i + step[i]) % count) for i in range(count)])


class Band:
    def __init__(self, rows, width, band):
        self.rows = rows
        self.width = width
        self.band = band
        self.reach = reach = (band - 1) // 2
        corner = [(k, j) for k in range(-1, -reach - 1, -1) for j in range(0, k + reach + 1)]
        self.first = [b for b in corner if b[0] > -reach]
        self.second = [b for b in corner if b[0] == -reach] + [(k, -1) for k in range(-1, -reach - 1, -1)]
        self.rest = [(k, j) for j in range(-2, -reach - 1, -1) for k in range(-1, -reach - 1, -1)]
        self.targets = [(i, j) for i in range(reach) for j in range(i - reach, reach)]
        self.last_targets = [t for t in self.targets if t[1] < -1]
        self.second_targets = [t for t in self.targets if t[1] == -1 or t == (0, 0)]
        self.first_targets = [t for t in self.targets if t[1] >= 0 and t != (0, 0)]

    def row(self, side, i):
        return i + side * (self.rows - 1 - 2 * i)

    def slot(self, side, i, j):
        return self.reach + (1 - 2 * side) * (j - i)

    def cols(self, slot, count=1):
        start = slot * self.width
        return pl.ds(start if isinstance(start, int) else pl.multiple_of(start, self.width), count * self.width)

    def sent(self, side, block):
        k, j = block
        return (1 - side) * (k + self.rows) + side * (-1 - k), self.slot(side, k, j)

    def inner(self, i, j, low, high):
        return range(max(low, i - self.reach, j - self.reach), min(high, i + self.reach, j + self.reach) + 1)


def dot(a, b):
    return jnp.dot(a, b, preferred_element_type=F32)


def add(total, part):
    return part if total is None else total + part


def spec(space):
    return pl.BlockSpec(memory_space=space)


def in_hbm(x):
    return pltpu.with_memory_space_constraint(x, pltpu.HBM)


def call(kernel, ins, outs, scratch, args, aliases=None, flops=0, name=None):
    moved = sum(a.size * a.dtype.itemsize for a in args) + sum(o.size * o.dtype.itemsize for o, _ in outs)
    return pl.pallas_call(
        kernel,
        out_shape=[o for o, _ in outs],
        in_specs=[spec(space) for space in ins],
        out_specs=[spec(space) for _, space in outs],
        scratch_shapes=scratch,
        input_output_aliases=aliases or {},
        compiler_params=pltpu.CompilerParams(vmem_limit_bytes=VMEM_BYTES),
        cost_estimate=pl.CostEstimate(flops=flops, bytes_accessed=moved, transcendentals=0),
        name=name,
    )(*args)


def pack(g, link, blocks, mask, density):
    width = g.width

    def kernel(mask_ref, density_ref, out, marks, mark_sem, sems):
        theirs = 1 - neighbour_side(link)
        mark = pltpu.make_async_copy(mask_ref, marks, mark_sem)
        mark.start()
        copies = []
        for n, block in enumerate(blocks):
            row, slot = g.sent(theirs, block)
            copies.append(pltpu.make_async_copy(density_ref.at[row, :, g.cols(slot)], out.at[n], sems.at[n]))
            copies[-1].start()
        mark.wait()
        for n, block in enumerate(blocks):
            copies[n].wait()
            row, slot = g.sent(theirs, block)

            @pl.when(marks[row, slot] == 0)
            def _():
                out[n] = jnp.zeros((width, width), BF16)

    return call(
        kernel,
        [pltpu.HBM, pltpu.HBM],
        [(jax.ShapeDtypeStruct((len(blocks), width, width), BF16), pltpu.VMEM)],
        [
            pltpu.SMEM(mask.shape, jnp.int32),
            pltpu.SemaphoreType.DMA,
            pltpu.SemaphoreType.DMA((len(blocks),)),
        ],
        (in_hbm(mask), in_hbm(density)),
        name="pack",
    )[0]


def local(g, near_blocks, mask, density):
    rows, width, strip = density.shape
    reach, band = g.reach, g.band

    def kernel(mask_ref, density_ref, out_ref, own, sums, near, done, in_sems, out_sems, near_sems):
        loads = [pltpu.make_async_copy(density_ref.at[r], own.at[r], in_sems.at[r]) for r in range(rows)]
        for load in loads:
            load.start()
        for r in range(rows):
            loads[r].wait()
            for s in range(band):

                @pl.when(mask_ref[r, s] == 0)
                def _():
                    own[r, :, g.cols(s)] = jnp.zeros((width, width), BF16)

        stores = []
        for n, block in enumerate(near_blocks):
            row, slot = g.sent(1 - neighbour_side(NEAR), block)
            stores.append(pltpu.make_async_copy(own.at[row, :, g.cols(slot)], near.at[n], near_sems.at[n]))
            stores[-1].start()
        for i in range(rows):
            side = 0 if 2 * i < rows else 1
            final = max(0, band - 2 * reach + g.row(side, i))
            for s in range(band):
                j = i + s - reach
                total = None
                for k in g.inner(i, j, 0, rows - 1):
                    total = add(total, dot(own[i, :, g.cols(k - i + reach)], own[k, :, g.cols(j - k + reach)]))
                ends = s >= band - final if side == 0 else s < final
                if ends:
                    done[i, :, g.cols(s)] = jnp.where(mask_ref[i, s] == 0, 0.0, total).astype(BF16)
                else:
                    sums[i, :, g.cols(s)] = total
            give = g.cols(band - final, final) if side == 0 else g.cols(0, final)
            stores.append(pltpu.make_async_copy(done.at[i, :, give], out_ref.at[i, :, give], out_sems.at[i]))
            stores[-1].start()
        for store in stores:
            store.wait()

    return call(
        kernel,
        [pltpu.SMEM, pltpu.HBM],
        [
            (jax.ShapeDtypeStruct(density.shape, BF16), pltpu.HBM),
            (jax.ShapeDtypeStruct(density.shape, BF16), pltpu.VMEM),
            (jax.ShapeDtypeStruct(density.shape, F32), pltpu.VMEM),
            (jax.ShapeDtypeStruct((len(near_blocks), width, width), BF16), pltpu.VMEM),
        ],
        [
            pltpu.VMEM(density.shape, BF16),
            pltpu.SemaphoreType.DMA((rows,)),
            pltpu.SemaphoreType.DMA((rows,)),
            pltpu.SemaphoreType.DMA((len(near_blocks),)),
        ],
        (mask, in_hbm(density)),
        flops=2 * 160 * width**3,
        name="local",
    )


def partials(g, link, own, first):
    width, reach = g.width, g.reach
    targets = g.last_targets

    def kernel(own_ref, halo_ref, out):
        theirs = 1 - neighbour_side(link)
        row_ids = lax.broadcasted_iota(jnp.int32, (CODE_ROWS, width), 0)
        powers = jnp.zeros((CODE_ROWS, width), F32)
        for n, (i, j) in enumerate(targets):
            total = None
            for k in g.inner(i, j, -reach, -1):
                row, slot = g.sent(theirs, (k, j))
                total = add(total, dot(halo_ref[g.first.index((-1 - i, -1 - k))], own_ref[row, :, g.cols(slot)]))
            top = jnp.maximum(jnp.max(jnp.abs(total), axis=0, keepdims=True), 2.0**-100)
            power = jnp.ceil(jnp.log2(top) + 0.001)
            code = jnp.round(total * jnp.exp2(CODE_BITS - power))
            out[pl.ds(n * width, width), :] = code.astype(jnp.int32).astype(jnp.int16)
            powers = jnp.where(row_ids == n, power, powers)
        out[pl.ds(len(targets) * width, CODE_ROWS), :] = powers.astype(jnp.int32).astype(jnp.int16)

    return call(
        kernel,
        [pltpu.VMEM] * 2,
        [(jax.ShapeDtypeStruct((len(targets) * width + CODE_ROWS, width), jnp.int16), pltpu.VMEM)],
        [],
        (own, first),
        flops=2 * 8 * width**3,
        name="partials",
    )[0]


def finish(g, link, targets, mask, sums, out, term_of, operands, flops, name):
    width = g.width
    nt, nops = len(targets), len(operands)

    def kernel(mask_ref, sum_ref, *refs):
        ins, (out_ref, done, sems) = refs[:nops], refs[nops + 1 :]
        side = neighbour_side(link)
        stores = []
        for n, (i, j) in enumerate(targets):
            row, slot = g.row(side, i), g.slot(side, i, j)
            value = sum_ref[row, :, g.cols(slot)] + term_of(ins, side, i, j)
            done[n] = jnp.where(mask_ref[row, slot] == 0, 0.0, value).astype(BF16)
            stores.append(pltpu.make_async_copy(done.at[n], out_ref.at[row, :, g.cols(slot)], sems.at[n]))
            stores[-1].start()
        for store in stores:
            store.wait()

    return call(
        kernel,
        [pltpu.SMEM] + [pltpu.VMEM] * (1 + nops) + [pltpu.HBM],
        [(jax.ShapeDtypeStruct(out.shape, out.dtype), pltpu.HBM)],
        [
            pltpu.VMEM((nt, width, width), BF16),
            pltpu.SemaphoreType.DMA((nt,)),
        ],
        (mask, sums, *operands, out),
        aliases={2 + nops: 0},
        flops=flops,
        name=name,
    )[0]


def with_halo(g, link, targets, lists, mask, own, sums, halos, out, name):
    where = {b: (p, n) for p, part in enumerate(lists) for n, b in enumerate(part)}

    def inner(i, j):
        return [k for k in g.inner(i, j, -g.reach, -1) if (k, j) in where]

    def term_of(ins, side, i, j):
        total = None
        for k in inner(i, j):
            p, n = where[k, j]
            total = add(total, dot(ins[0][g.row(side, i), :, g.cols(g.slot(side, i, k))], ins[1 + p][n]))
        return total

    flops = WEIGHT * 2 * sum(len(inner(i, j)) for i, j in targets) * g.width**3
    return finish(g, link, targets, mask, sums, out, term_of, (own, *halos), flops, name)


def with_partials(g, link, mask, sums, coded, out):
    width, targets = g.width, g.last_targets

    def term_of(ins, side, i, j):
        n = targets.index((i, j))
        code = ins[0][pl.ds(n * width, width), :].astype(jnp.int32).astype(F32)
        power = ins[0][pl.ds(len(targets) * width, CODE_ROWS), :].astype(jnp.int32).astype(F32)[n : n + 1]
        return code * jnp.exp2(power - CODE_BITS)

    return finish(g, link, targets, mask, sums, out, term_of, (coded,), 0, "last")


def on_device(density, block_mask):
    rows, width, strip = density.shape
    g = Band(rows, width, block_mask.shape[1])
    mask = block_mask
    near_blocks = g.first + g.second + g.rest

    first = exchange(pack(g, FAR, g.first, mask, density), FAR)
    packed_second = pack(g, FAR, g.second, mask, density)
    second = exchange(packed_second, FAR)
    later, _ = lax.optimization_barrier((mask, packed_second))
    out, own, sums, near = local(g, near_blocks, later, density)
    near = exchange(near, NEAR)
    coded = exchange(partials(g, FAR, own, first), FAR)
    out = with_halo(g, FAR, g.first_targets, [g.first], mask, own, sums, [first], out, "corner")
    out = with_halo(g, NEAR, g.targets, [near_blocks], mask, own, sums, [near], out, "near")
    out = with_halo(g, FAR, g.second_targets, [g.first, g.second], mask, own, sums, [first, second], out, "edge")
    return with_partials(g, FAR, mask, sums, coded, out)


def solution(mesh):
    in_specs = (P(("groups", "grid"), None, None), P(("groups", "grid"), None))
    out_specs = P(("groups", "grid"), None, None)
    return jax.shard_map(on_device, mesh=mesh, in_specs=in_specs, out_specs=out_specs, check_vma=False)
```

```python
import jax
import jax.numpy as jnp
from jax import lax
from jax.experimental import pallas as pl
from jax.experimental.pallas import tpu as pltpu
from jax.sharding import PartitionSpec as P

F32 = jnp.float32
BF16 = jnp.bfloat16
VMEM_BYTES = 26 * 1024 * 1024
CODE_BITS = 15
WEIGHT = 100
CODE_ROWS = 16
FAR, NEAR = 0, 1


def neighbour_side(link):
    odd = lax.rem(lax.axis_index("grid"), 2)
    return odd if link == FAR else 1 - odd


def exchange(x, link):
    count = lax.axis_size("grid")
    step = [1 if (i % 2 == 0) == (link == NEAR) else -1 for i in range(count)]
    return lax.ppermute(x, "grid", [(i, (i + step[i]) % count) for i in range(count)])


class Band:
    def __init__(self, rows, width, band):
        self.rows = rows
        self.width = width
        self.band = band
        self.reach = reach = (band - 1) // 2
        corner = [(k, j) for k in range(-1, -reach - 1, -1) for j in range(0, k + reach + 1)]
        self.first = [b for b in corner if b[0] > -reach]
        self.second = [b for b in corner if b[0] == -reach] + [(k, -1) for k in range(-1, -reach - 1, -1)]
        self.rest = [(k, j) for j in range(-2, -reach - 1, -1) for k in range(-1, -reach - 1, -1)]
        self.targets = [(i, j) for i in range(reach) for j in range(i - reach, reach)]
        self.last_targets = [t for t in self.targets if t[1] < -1]
        self.second_targets = [t for t in self.targets if t[1] == -1 or t == (0, 0)]
        self.first_targets = [t for t in self.targets if t[1] >= 0 and t != (0, 0)]

    def row(self, side, i):
        return i + side * (self.rows - 1 - 2 * i)

    def slot(self, side, i, j):
        return self.reach + (1 - 2 * side) * (j - i)

    def cols(self, slot, count=1):
        start = slot * self.width
        return pl.ds(start if isinstance(start, int) else pl.multiple_of(start, self.width), count * self.width)

    def sent(self, side, block):
        k, j = block
        return (1 - side) * (k + self.rows) + side * (-1 - k), self.slot(side, k, j)

    def inner(self, i, j, low, high):
        return range(max(low, i - self.reach, j - self.reach), min(high, i + self.reach, j + self.reach) + 1)


def dot(a, b):
    return jnp.dot(a, b, preferred_element_type=F32)


def add(total, part):
    return part if total is None else total + part


def spec(space):
    return pl.BlockSpec(memory_space=space)


def in_hbm(x):
    return pltpu.with_memory_space_constraint(x, pltpu.HBM)


def call(kernel, ins, outs, scratch, args, aliases=None, flops=0, name=None):
    moved = sum(a.size * a.dtype.itemsize for a in args) + sum(o.size * o.dtype.itemsize for o, _ in outs)
    return pl.pallas_call(
        kernel,
        out_shape=[o for o, _ in outs],
        in_specs=[spec(space) for space in ins],
        out_specs=[spec(space) for _, space in outs],
        scratch_shapes=scratch,
        input_output_aliases=aliases or {},
        compiler_params=pltpu.CompilerParams(vmem_limit_bytes=VMEM_BYTES),
        cost_estimate=pl.CostEstimate(flops=flops, bytes_accessed=moved, transcendentals=0),
        name=name,
    )(*args)


def pack(g, link, blocks, mask, density):
    width = g.width

    def kernel(mask_ref, density_ref, out, marks, mark_sem, sems):
        theirs = 1 - neighbour_side(link)
        mark = pltpu.make_async_copy(mask_ref, marks, mark_sem)
        mark.start()
        copies = []
        for n, block in enumerate(blocks):
            row, slot = g.sent(theirs, block)
            copies.append(pltpu.make_async_copy(density_ref.at[row, :, g.cols(slot)], out.at[n], sems.at[n]))
            copies[-1].start()
        mark.wait()
        for n, block in enumerate(blocks):
            copies[n].wait()
            row, slot = g.sent(theirs, block)

            @pl.when(marks[row, slot] == 0)
            def _():
                out[n] = jnp.zeros((width, width), BF16)

    return call(
        kernel,
        [pltpu.HBM, pltpu.HBM],
        [(jax.ShapeDtypeStruct((len(blocks), width, width), BF16), pltpu.VMEM)],
        [
            pltpu.SMEM(mask.shape, jnp.int32),
            pltpu.SemaphoreType.DMA,
            pltpu.SemaphoreType.DMA((len(blocks),)),
        ],
        (in_hbm(mask), in_hbm(density)),
        name="pack",
    )[0]


def local(g, near_blocks, mask, density):
    rows, width, strip = density.shape
    reach, band = g.reach, g.band

    def kernel(mask_ref, density_ref, out_ref, own, sums, near, gates, done, in_sems, out_sems, near_sems):
        loads = [pltpu.make_async_copy(density_ref.at[r], own.at[r], in_sems.at[r]) for r in range(rows)]
        for load in loads:
            load.start()
        for r in range(rows):
            loads[r].wait()
            for s in range(band):

                @pl.when(mask_ref[r, s] == 0)
                def _():
                    own[r, :, g.cols(s)] = jnp.zeros((width, width), BF16)

                gates[r * band + s] = jnp.full((1, width), mask_ref[r, s].astype(F32))

        stores = []
        for n, block in enumerate(near_blocks):
            row, slot = g.sent(1 - neighbour_side(NEAR), block)
            stores.append(pltpu.make_async_copy(own.at[row, :, g.cols(slot)], near.at[n], near_sems.at[n]))
            stores[-1].start()
        for i in range(rows):
            side = 0 if 2 * i < rows else 1
            final = max(0, band - 2 * reach + g.row(side, i))
            for s in range(band):
                j = i + s - reach
                total = None
                for k in g.inner(i, j, 0, rows - 1):
                    total = add(total, dot(own[i, :, g.cols(k - i + reach)], own[k, :, g.cols(j - k + reach)]))
                ends = s >= band - final if side == 0 else s < final
                if ends:
                    done[i, :, g.cols(s)] = jnp.where(mask_ref[i, s] == 0, 0.0, total).astype(BF16)
                else:
                    sums[i, :, g.cols(s)] = total
            give = g.cols(band - final, final) if side == 0 else g.cols(0, final)
            stores.append(pltpu.make_async_copy(done.at[i, :, give], out_ref.at[i, :, give], out_sems.at[i]))
            stores[-1].start()
        for store in stores:
            store.wait()

    return call(
        kernel,
        [pltpu.SMEM, pltpu.HBM],
        [
            (jax.ShapeDtypeStruct(density.shape, BF16), pltpu.HBM),
            (jax.ShapeDtypeStruct(density.shape, BF16), pltpu.VMEM),
            (jax.ShapeDtypeStruct(density.shape, F32), pltpu.VMEM),
            (jax.ShapeDtypeStruct((len(near_blocks), width, width), BF16), pltpu.VMEM),
            (jax.ShapeDtypeStruct((rows * band, 1, width), F32), pltpu.VMEM),
        ],
        [
            pltpu.VMEM(density.shape, BF16),
            pltpu.SemaphoreType.DMA((rows,)),
            pltpu.SemaphoreType.DMA((rows,)),
            pltpu.SemaphoreType.DMA((len(near_blocks),)),
        ],
        (mask, in_hbm(density)),
        flops=2 * 160 * width**3,
        name="local",
    )


def partials(g, link, own, first):
    width, reach = g.width, g.reach
    targets = g.last_targets

    def kernel(own_ref, halo_ref, out):
        theirs = 1 - neighbour_side(link)
        row_ids = lax.broadcasted_iota(jnp.int32, (CODE_ROWS, width), 0)
        powers = jnp.zeros((CODE_ROWS, width), F32)
        for n, (i, j) in enumerate(targets):
            total = None
            for k in g.inner(i, j, -reach, -1):
                row, slot = g.sent(theirs, (k, j))
                total = add(total, dot(halo_ref[g.first.index((-1 - i, -1 - k))], own_ref[row, :, g.cols(slot)]))
            top = jnp.maximum(jnp.max(jnp.abs(total), axis=0, keepdims=True), 2.0**-100)
            power = jnp.ceil(jnp.log2(top) + 0.001)
            code = jnp.round(total * jnp.exp2(CODE_BITS - power))
            out[pl.ds(n * width, width), :] = code.astype(jnp.int32).astype(jnp.int16)
            powers = jnp.where(row_ids == n, power, powers)
        out[pl.ds(len(targets) * width, CODE_ROWS), :] = powers.astype(jnp.int32).astype(jnp.int16)

    return call(
        kernel,
        [pltpu.VMEM] * 2,
        [(jax.ShapeDtypeStruct((len(targets) * width + CODE_ROWS, width), jnp.int16), pltpu.VMEM)],
        [],
        (own, first),
        flops=2 * 8 * width**3,
        name="partials",
    )[0]


def finish(g, link, targets, gates, sums, out, term_of, operands, flops, name, chunk):
    width = g.width
    nt, nops = len(targets), len(operands)

    def kernel(gate_ref, sum_ref, *refs):
        ins, (out_ref, done, sems) = refs[:nops], refs[nops + 1 :]
        side = neighbour_side(link)
        stores = []
        for n, (i, j) in enumerate(targets):
            row, slot = g.row(side, i), g.slot(side, i, j)
            gate = gate_ref[row * g.band + slot]

            def some(start):
                lines = pl.ds(start, chunk)
                value = sum_ref[row, lines, g.cols(slot)] + term_of(ins, side, i, j, start)
                done[n, lines, :] = (value * gate).astype(BF16)

            if chunk == width:
                some(0)
            else:
                pl.loop(0, width, step=chunk)(some)
            stores.append(pltpu.make_async_copy(done.at[n], out_ref.at[row, :, g.cols(slot)], sems.at[n]))
            stores[-1].start()
        for store in stores:
            store.wait()

    return call(
        kernel,
        [pltpu.VMEM] * (2 + nops) + [pltpu.HBM],
        [(jax.ShapeDtypeStruct(out.shape, out.dtype), pltpu.HBM)],
        [
            pltpu.VMEM((nt, width, width), BF16),
            pltpu.SemaphoreType.DMA((nt,)),
        ],
        (gates, sums, *operands, out),
        aliases={2 + nops: 0},
        flops=flops,
        name=name,
    )[0]


def with_halo(g, link, targets, lists, gates, own, sums, halos, out, name):
    where = {b: (p, n) for p, part in enumerate(lists) for n, b in enumerate(part)}

    def inner(i, j):
        return [k for k in g.inner(i, j, -g.reach, -1) if (k, j) in where]

    def term_of(ins, side, i, j, start):
        total = None
        for k in inner(i, j):
            p, n = where[k, j]
            total = add(total, dot(ins[0][g.row(side, i), :, g.cols(g.slot(side, i, k))], ins[1 + p][n]))
        return total

    flops = WEIGHT * 2 * sum(len(inner(i, j)) for i, j in targets) * g.width**3
    return finish(g, link, targets, gates, sums, out, term_of, (own, *halos), flops, name, g.width)


def with_partials(g, link, gates, sums, coded, out):
    width, targets = g.width, g.last_targets

    chunk = width // 4

    def term_of(ins, side, i, j, start):
        n = targets.index((i, j))
        lines = pl.ds(pl.multiple_of(n * width + start, chunk), chunk)
        code = ins[0][lines, :].astype(jnp.int32).astype(F32)
        power = ins[0][pl.ds(len(targets) * width, CODE_ROWS), :].astype(jnp.int32).astype(F32)[n : n + 1]
        return code * jnp.exp2(power - CODE_BITS)

    return finish(g, link, targets, gates, sums, out, term_of, (coded,), 0, "last", chunk)


def on_device(density, block_mask):
    rows, width, strip = density.shape
    g = Band(rows, width, block_mask.shape[1])
    mask = block_mask
    near_blocks = g.first + g.second + g.rest

    first = exchange(pack(g, FAR, g.first, mask, density), FAR)
    packed_second = pack(g, FAR, g.second, mask, density)
    second = exchange(packed_second, FAR)
    later, _ = lax.optimization_barrier((mask, packed_second))
    out, own, sums, near, gates = local(g, near_blocks, later, density)
    near = exchange(near, NEAR)
    coded = exchange(partials(g, FAR, own, first), FAR)
    out = with_halo(g, FAR, g.first_targets, [g.first], gates, own, sums, [first], out, "corner")
    out = with_halo(g, NEAR, g.targets, [near_blocks], gates, own, sums, [near], out, "near")
    out = with_halo(g, FAR, g.second_targets, [g.first, g.second], gates, own, sums, [first, second], out, "edge")
    return with_partials(g, FAR, gates, sums, coded, out)


def solution(mesh):
    in_specs = (P(("groups", "grid"), None, None), P(("groups", "grid"), None))
    out_specs = P(("groups", "grid"), None, None)
    return jax.shard_map(on_device, mesh=mesh, in_specs=in_specs, out_specs=out_specs, check_vma=False)
```

```python
import jax
import jax.numpy as jnp
from jax import lax
from jax.experimental import pallas as pl
from jax.experimental.pallas import tpu as pltpu
from jax.sharding import PartitionSpec as P

F32 = jnp.float32
BF16 = jnp.bfloat16
VMEM_BYTES = 26 * 1024 * 1024
CODE_BITS = 15
WEIGHT = 100
CODE_ROWS = 16
FAR, NEAR = 0, 1


def neighbour_side(link):
    odd = lax.rem(lax.axis_index("grid"), 2)
    return odd if link == FAR else 1 - odd


def exchange(x, link):
    count = lax.axis_size("grid")
    step = [1 if (i % 2 == 0) == (link == NEAR) else -1 for i in range(count)]
    return lax.ppermute(x, "grid", [(i, (i + step[i]) % count) for i in range(count)])


class Band:
    def __init__(self, rows, width, band):
        self.rows = rows
        self.width = width
        self.band = band
        self.reach = reach = (band - 1) // 2
        corner = [(k, j) for k in range(-1, -reach - 1, -1) for j in range(0, k + reach + 1)]
        self.first = [b for b in corner if b[0] > -reach]
        self.second = [b for b in corner if b[0] == -reach] + [(k, -1) for k in range(-1, -reach - 1, -1)]
        self.rest = [(k, j) for j in range(-2, -reach - 1, -1) for k in range(-1, -reach - 1, -1)]
        self.targets = [(i, j) for i in range(reach) for j in range(i - reach, reach)]
        self.last_targets = [t for t in self.targets if t[1] < -1]
        self.second_targets = [t for t in self.targets if t[1] == -1 or t == (0, 0)]
        self.first_targets = [t for t in self.targets if t[1] >= 0 and t != (0, 0)]

    def row(self, side, i):
        return i + side * (self.rows - 1 - 2 * i)

    def slot(self, side, i, j):
        return self.reach + (1 - 2 * side) * (j - i)

    def cols(self, slot, count=1):
        start = slot * self.width
        return pl.ds(start if isinstance(start, int) else pl.multiple_of(start, self.width), count * self.width)

    def sent(self, side, block):
        k, j = block
        return (1 - side) * (k + self.rows) + side * (-1 - k), self.slot(side, k, j)

    def inner(self, i, j, low, high):
        return range(max(low, i - self.reach, j - self.reach), min(high, i + self.reach, j + self.reach) + 1)


def dot(a, b):
    return jnp.dot(a, b, preferred_element_type=F32)


def add(total, part):
    return part if total is None else total + part


def spec(space):
    return pl.BlockSpec(memory_space=space)


def in_hbm(x):
    return pltpu.with_memory_space_constraint(x, pltpu.HBM)


def call(kernel, ins, outs, scratch, args, aliases=None, flops=0, name=None):
    moved = sum(a.size * a.dtype.itemsize for a in args) + sum(o.size * o.dtype.itemsize for o, _ in outs)
    return pl.pallas_call(
        kernel,
        out_shape=[o for o, _ in outs],
        in_specs=[spec(space) for space in ins],
        out_specs=[spec(space) for _, space in outs],
        scratch_shapes=scratch,
        input_output_aliases=aliases or {},
        compiler_params=pltpu.CompilerParams(vmem_limit_bytes=VMEM_BYTES),
        cost_estimate=pl.CostEstimate(flops=flops, bytes_accessed=moved, transcendentals=0),
        name=name,
    )(*args)


def pack(g, link, blocks, mask, density):
    width = g.width

    def kernel(mask_ref, density_ref, out, marks, mark_sem, sems):
        theirs = 1 - neighbour_side(link)
        mark = pltpu.make_async_copy(mask_ref, marks, mark_sem)
        mark.start()
        copies = []
        for n, block in enumerate(blocks):
            row, slot = g.sent(theirs, block)
            copies.append(pltpu.make_async_copy(density_ref.at[row, :, g.cols(slot)], out.at[n], sems.at[n]))
            copies[-1].start()
        mark.wait()
        for n, block in enumerate(blocks):
            copies[n].wait()
            row, slot = g.sent(theirs, block)

            @pl.when(marks[row, slot] == 0)
            def _():
                out[n] = jnp.zeros((width, width), BF16)

    return call(
        kernel,
        [pltpu.HBM, pltpu.HBM],
        [(jax.ShapeDtypeStruct((len(blocks), width, width), BF16), pltpu.VMEM)],
        [
            pltpu.SMEM(mask.shape, jnp.int32),
            pltpu.SemaphoreType.DMA,
            pltpu.SemaphoreType.DMA((len(blocks),)),
        ],
        (in_hbm(mask), in_hbm(density)),
        name="pack",
    )[0]


def local(g, near_blocks, mask, density):
    rows, width, strip = density.shape
    reach, band = g.reach, g.band

    def kernel(mask_ref, density_ref, out_ref, own, sums, near, gates, done, in_sems, out_sems, near_sems):
        loads = [pltpu.make_async_copy(density_ref.at[r], own.at[r], in_sems.at[r]) for r in range(rows)]
        for load in loads:
            load.start()
        for r in range(rows):
            loads[r].wait()
            for s in range(band):

                @pl.when(mask_ref[r, s] == 0)
                def _():
                    own[r, :, g.cols(s)] = jnp.zeros((width, width), BF16)

                gates[r * band + s] = jnp.full((1, width), mask_ref[r, s].astype(F32))

        stores = []
        for n, block in enumerate(near_blocks):
            row, slot = g.sent(1 - neighbour_side(NEAR), block)
            stores.append(pltpu.make_async_copy(own.at[row, :, g.cols(slot)], near.at[n], near_sems.at[n]))
            stores[-1].start()
        for i in range(rows):
            side = 0 if 2 * i < rows else 1
            final = max(0, band - 2 * reach + g.row(side, i))
            for s in range(band):
                j = i + s - reach
                total = None
                for k in g.inner(i, j, 0, rows - 1):
                    total = add(total, dot(own[i, :, g.cols(k - i + reach)], own[k, :, g.cols(j - k + reach)]))
                ends = s >= band - final if side == 0 else s < final
                if ends:
                    done[i, :, g.cols(s)] = jnp.where(mask_ref[i, s] == 0, 0.0, total).astype(BF16)
                else:
                    sums[i, :, g.cols(s)] = total
            give = g.cols(band - final, final) if side == 0 else g.cols(0, final)
            stores.append(pltpu.make_async_copy(done.at[i, :, give], out_ref.at[i, :, give], out_sems.at[i]))
            stores[-1].start()
        for store in stores:
            store.wait()

    return call(
        kernel,
        [pltpu.SMEM, pltpu.HBM],
        [
            (jax.ShapeDtypeStruct(density.shape, BF16), pltpu.HBM),
            (jax.ShapeDtypeStruct(density.shape, BF16), pltpu.VMEM),
            (jax.ShapeDtypeStruct(density.shape, F32), pltpu.VMEM),
            (jax.ShapeDtypeStruct((len(near_blocks), width, width), BF16), pltpu.VMEM),
            (jax.ShapeDtypeStruct((rows * band, 1, width), F32), pltpu.VMEM),
        ],
        [
            pltpu.VMEM(density.shape, BF16),
            pltpu.SemaphoreType.DMA((rows,)),
            pltpu.SemaphoreType.DMA((rows,)),
            pltpu.SemaphoreType.DMA((len(near_blocks),)),
        ],
        (mask, in_hbm(density)),
        flops=2 * 160 * width**3,
        name="local",
    )


def partials(g, link, own, first):
    width, reach = g.width, g.reach
    targets = g.last_targets

    def kernel(own_ref, halo_ref, out):
        theirs = 1 - neighbour_side(link)
        row_ids = lax.broadcasted_iota(jnp.int32, (CODE_ROWS, width), 0)
        powers = jnp.zeros((CODE_ROWS, width), F32)
        for n, (i, j) in enumerate(targets):
            total = None
            for k in g.inner(i, j, -reach, -1):
                row, slot = g.sent(theirs, (k, j))
                total = add(total, dot(halo_ref[g.first.index((-1 - i, -1 - k))], own_ref[row, :, g.cols(slot)]))
            top = jnp.maximum(jnp.max(jnp.abs(total), axis=0, keepdims=True), 2.0**-100)
            power = jnp.ceil(jnp.log2(top) + 0.001)
            code = jnp.round(total * jnp.exp2(CODE_BITS - power))
            out[pl.ds(n * width, width), :] = code.astype(jnp.int32).astype(jnp.int16)
            powers = jnp.where(row_ids == n, power, powers)
        out[pl.ds(len(targets) * width, CODE_ROWS), :] = powers.astype(jnp.int32).astype(jnp.int16)

    return call(
        kernel,
        [pltpu.VMEM] * 2,
        [(jax.ShapeDtypeStruct((len(targets) * width + CODE_ROWS, width), jnp.int16), pltpu.VMEM)],
        [],
        (own, first),
        flops=2 * 8 * width**3,
        name="partials",
    )[0]


def finish(g, link, targets, gates, sums, out, term_of, operands, flops, name, chunk):
    width = g.width
    nt, nops = len(targets), len(operands)

    def kernel(gate_ref, sum_ref, *refs):
        ins, (out_ref, done, sems) = refs[:nops], refs[nops + 1 :]
        side = neighbour_side(link)
        stores = []
        for n, (i, j) in enumerate(targets):
            row, slot = g.row(side, i), g.slot(side, i, j)
            gate = gate_ref[row * g.band + slot]

            def some(start):
                lines = pl.ds(start, chunk)
                value = sum_ref[row, lines, g.cols(slot)] + term_of(ins, side, i, j, start)
                done[n, lines, :] = (value * gate).astype(BF16)

            if chunk == width:
                some(0)
            else:
                pl.loop(0, width, step=chunk)(some)
            stores.append(pltpu.make_async_copy(done.at[n], out_ref.at[row, :, g.cols(slot)], sems.at[n]))
            stores[-1].start()
        for store in stores:
            store.wait()

    return call(
        kernel,
        [pltpu.VMEM] * (2 + nops) + [pltpu.HBM],
        [(jax.ShapeDtypeStruct(out.shape, out.dtype), pltpu.HBM)],
        [
            pltpu.VMEM((nt, width, width), BF16),
            pltpu.SemaphoreType.DMA((nt,)),
        ],
        (gates, sums, *operands, out),
        aliases={2 + nops: 0},
        flops=flops,
        name=name,
    )[0]


def with_halo(g, link, targets, lists, gates, own, sums, halos, out, name):
    where = {b: (p, n) for p, part in enumerate(lists) for n, b in enumerate(part)}

    def inner(i, j):
        return [k for k in g.inner(i, j, -g.reach, -1) if (k, j) in where]

    def term_of(ins, side, i, j, start):
        total = None
        for k in inner(i, j):
            p, n = where[k, j]
            total = add(total, dot(ins[0][g.row(side, i), :, g.cols(g.slot(side, i, k))], ins[1 + p][n]))
        return total

    flops = WEIGHT * 2 * sum(len(inner(i, j)) for i, j in targets) * g.width**3
    return finish(g, link, targets, gates, sums, out, term_of, (own, *halos), flops, name, g.width)


def with_partials(g, link, gates, sums, coded, out):
    width, targets = g.width, g.last_targets

    chunk = width

    def term_of(ins, side, i, j, start):
        n = targets.index((i, j))
        lines = pl.ds(pl.multiple_of(n * width + start, chunk), chunk)
        code = ins[0][lines, :].astype(jnp.int32).astype(F32)
        power = ins[0][pl.ds(len(targets) * width, CODE_ROWS), :].astype(jnp.int32).astype(F32)[n : n + 1]
        return code * jnp.exp2(power - CODE_BITS)

    return finish(g, link, targets, gates, sums, out, term_of, (coded,), 0, "last", chunk)


def on_device(density, block_mask):
    rows, width, strip = density.shape
    g = Band(rows, width, block_mask.shape[1])
    mask = block_mask
    near_blocks = g.first + g.second + g.rest

    first = exchange(pack(g, FAR, g.first, mask, density), FAR)
    packed_second = pack(g, FAR, g.second, mask, density)
    second = exchange(packed_second, FAR)
    later, _ = lax.optimization_barrier((mask, packed_second))
    out, own, sums, near, gates = local(g, near_blocks, later, density)
    near = exchange(near, NEAR)
    coded = exchange(partials(g, FAR, own, first), FAR)
    out = with_halo(g, FAR, g.first_targets, [g.first], gates, own, sums, [first], out, "corner")
    out = with_halo(g, NEAR, g.targets, [near_blocks], gates, own, sums, [near], out, "near")
    out = with_halo(g, FAR, g.second_targets, [g.first, g.second], gates, own, sums, [first, second], out, "edge")
    return with_partials(g, FAR, gates, sums, coded, out)


def solution(mesh):
    in_specs = (P(("groups", "grid"), None, None), P(("groups", "grid"), None))
    out_specs = P(("groups", "grid"), None, None)
    return jax.shard_map(on_device, mesh=mesh, in_specs=in_specs, out_specs=out_specs, check_vma=False)
```

```python
import jax
import jax.numpy as jnp
from jax import lax
from jax.experimental import pallas as pl
from jax.experimental.pallas import tpu as pltpu
from jax.sharding import PartitionSpec as P

F32 = jnp.float32
BF16 = jnp.bfloat16
VMEM_BYTES = 26 * 1024 * 1024
CODE_BITS = 15
WEIGHT = 150
CODE_ROWS = 16
FAR, NEAR = 0, 1


def neighbour_side(link):
    odd = lax.rem(lax.axis_index("grid"), 2)
    return odd if link == FAR else 1 - odd


def exchange(x, link):
    count = lax.axis_size("grid")
    step = [1 if (i % 2 == 0) == (link == NEAR) else -1 for i in range(count)]
    return lax.ppermute(x, "grid", [(i, (i + step[i]) % count) for i in range(count)])


class Band:
    def __init__(self, rows, width, band):
        self.rows = rows
        self.width = width
        self.band = band
        self.reach = reach = (band - 1) // 2
        corner = [(k, j) for k in range(-1, -reach - 1, -1) for j in range(0, k + reach + 1)]
        self.first = [b for b in corner if b[0] > -reach]
        self.second = [b for b in corner if b[0] == -reach] + [(k, -1) for k in range(-1, -reach - 1, -1)]
        self.rest = [(k, j) for j in range(-2, -reach - 1, -1) for k in range(-1, -reach - 1, -1)]
        self.targets = [(i, j) for i in range(reach) for j in range(i - reach, reach)]
        self.last_targets = [t for t in self.targets if t[1] < -1]
        self.second_targets = [t for t in self.targets if t[1] == -1 or t == (0, 0)]
        self.first_targets = [t for t in self.targets if t[1] >= 0 and t != (0, 0)]

    def row(self, side, i):
        return i + side * (self.rows - 1 - 2 * i)

    def slot(self, side, i, j):
        return self.reach + (1 - 2 * side) * (j - i)

    def cols(self, slot, count=1):
        start = slot * self.width
        return pl.ds(start if isinstance(start, int) else pl.multiple_of(start, self.width), count * self.width)

    def sent(self, side, block):
        k, j = block
        return (1 - side) * (k + self.rows) + side * (-1 - k), self.slot(side, k, j)

    def inner(self, i, j, low, high):
        return range(max(low, i - self.reach, j - self.reach), min(high, i + self.reach, j + self.reach) + 1)


def dot(a, b):
    return jnp.dot(a, b, preferred_element_type=F32)


def add(total, part):
    return part if total is None else total + part


def spec(space):
    return pl.BlockSpec(memory_space=space)


def in_hbm(x):
    return pltpu.with_memory_space_constraint(x, pltpu.HBM)


def call(kernel, ins, outs, scratch, args, aliases=None, flops=0, name=None):
    moved = sum(a.size * a.dtype.itemsize for a in args) + sum(o.size * o.dtype.itemsize for o, _ in outs)
    return pl.pallas_call(
        kernel,
        out_shape=[o for o, _ in outs],
        in_specs=[spec(space) for space in ins],
        out_specs=[spec(space) for _, space in outs],
        scratch_shapes=scratch,
        input_output_aliases=aliases or {},
        compiler_params=pltpu.CompilerParams(vmem_limit_bytes=VMEM_BYTES),
        cost_estimate=pl.CostEstimate(flops=flops, bytes_accessed=moved, transcendentals=0),
        name=name,
    )(*args)


def pack(g, link, blocks, mask, density):
    width = g.width

    def kernel(mask_ref, density_ref, out, marks, mark_sem, sems):
        theirs = 1 - neighbour_side(link)
        mark = pltpu.make_async_copy(mask_ref, marks, mark_sem)
        mark.start()
        copies = []
        for n, block in enumerate(blocks):
            row, slot = g.sent(theirs, block)
            copies.append(pltpu.make_async_copy(density_ref.at[row, :, g.cols(slot)], out.at[n], sems.at[n]))
            copies[-1].start()
        mark.wait()
        for n, block in enumerate(blocks):
            copies[n].wait()
            row, slot = g.sent(theirs, block)

            @pl.when(marks[row, slot] == 0)
            def _():
                out[n] = jnp.zeros((width, width), BF16)

    return call(
        kernel,
        [pltpu.HBM, pltpu.HBM],
        [(jax.ShapeDtypeStruct((len(blocks), width, width), BF16), pltpu.VMEM)],
        [
            pltpu.SMEM(mask.shape, jnp.int32),
            pltpu.SemaphoreType.DMA,
            pltpu.SemaphoreType.DMA((len(blocks),)),
        ],
        (in_hbm(mask), in_hbm(density)),
        name="pack",
    )[0]


def local(g, near_blocks, mask, density):
    rows, width, strip = density.shape
    reach, band = g.reach, g.band

    def kernel(mask_ref, density_ref, out_ref, own, sums, near, gates, done, in_sems, out_sems, near_sems):
        loads = [pltpu.make_async_copy(density_ref.at[r], own.at[r], in_sems.at[r]) for r in range(rows)]
        for load in loads:
            load.start()
        for r in range(rows):
            loads[r].wait()
            for s in range(band):

                @pl.when(mask_ref[r, s] == 0)
                def _():
                    own[r, :, g.cols(s)] = jnp.zeros((width, width), BF16)

                gates[r * band + s] = jnp.full((1, width), mask_ref[r, s].astype(F32))

        stores = []
        for n, block in enumerate(near_blocks):
            row, slot = g.sent(1 - neighbour_side(NEAR), block)
            stores.append(pltpu.make_async_copy(own.at[row, :, g.cols(slot)], near.at[n], near_sems.at[n]))
            stores[-1].start()
        for i in range(rows):
            side = 0 if 2 * i < rows else 1
            final = max(0, band - 2 * reach + g.row(side, i))
            for s in range(band):
                j = i + s - reach
                total = None
                for k in g.inner(i, j, 0, rows - 1):
                    total = add(total, dot(own[i, :, g.cols(k - i + reach)], own[k, :, g.cols(j - k + reach)]))
                ends = s >= band - final if side == 0 else s < final
                if ends:
                    done[i, :, g.cols(s)] = jnp.where(mask_ref[i, s] == 0, 0.0, total).astype(BF16)
                else:
                    sums[i, :, g.cols(s)] = total
            give = g.cols(band - final, final) if side == 0 else g.cols(0, final)
            stores.append(pltpu.make_async_copy(done.at[i, :, give], out_ref.at[i, :, give], out_sems.at[i]))
            stores[-1].start()
        for store in stores:
            store.wait()

    return call(
        kernel,
        [pltpu.SMEM, pltpu.HBM],
        [
            (jax.ShapeDtypeStruct(density.shape, BF16), pltpu.HBM),
            (jax.ShapeDtypeStruct(density.shape, BF16), pltpu.VMEM),
            (jax.ShapeDtypeStruct(density.shape, F32), pltpu.VMEM),
            (jax.ShapeDtypeStruct((len(near_blocks), width, width), BF16), pltpu.VMEM),
            (jax.ShapeDtypeStruct((rows * band, 1, width), F32), pltpu.VMEM),
        ],
        [
            pltpu.VMEM(density.shape, BF16),
            pltpu.SemaphoreType.DMA((rows,)),
            pltpu.SemaphoreType.DMA((rows,)),
            pltpu.SemaphoreType.DMA((len(near_blocks),)),
        ],
        (mask, in_hbm(density)),
        flops=2 * 160 * width**3,
        name="local",
    )


def partials(g, link, own, first):
    width, reach = g.width, g.reach
    targets = g.last_targets

    def kernel(own_ref, halo_ref, out):
        theirs = 1 - neighbour_side(link)
        row_ids = lax.broadcasted_iota(jnp.int32, (CODE_ROWS, width), 0)
        powers = jnp.zeros((CODE_ROWS, width), F32)
        for n, (i, j) in enumerate(targets):
            total = None
            for k in g.inner(i, j, -reach, -1):
                row, slot = g.sent(theirs, (k, j))
                total = add(total, dot(halo_ref[g.first.index((-1 - i, -1 - k))], own_ref[row, :, g.cols(slot)]))
            top = jnp.maximum(jnp.max(jnp.abs(total), axis=0, keepdims=True), 2.0**-100)
            power = jnp.ceil(jnp.log2(top) + 0.001)
            code = jnp.round(total * jnp.exp2(CODE_BITS - power))
            out[pl.ds(n * width, width), :] = code.astype(jnp.int32).astype(jnp.int16)
            powers = jnp.where(row_ids == n, power, powers)
        out[pl.ds(len(targets) * width, CODE_ROWS), :] = powers.astype(jnp.int32).astype(jnp.int16)

    return call(
        kernel,
        [pltpu.VMEM] * 2,
        [(jax.ShapeDtypeStruct((len(targets) * width + CODE_ROWS, width), jnp.int16), pltpu.VMEM)],
        [],
        (own, first),
        flops=WEIGHT * 2 * 8 * width**3,
        name="partials",
    )[0]


def finish(g, link, targets, gates, sums, out, term_of, operands, flops, name, chunk):
    width = g.width
    nt, nops = len(targets), len(operands)

    def kernel(gate_ref, sum_ref, *refs):
        ins, (out_ref, done, sems) = refs[:nops], refs[nops + 1 :]
        side = neighbour_side(link)
        stores = []
        for n, (i, j) in enumerate(targets):
            row, slot = g.row(side, i), g.slot(side, i, j)
            gate = gate_ref[row * g.band + slot]

            def some(start):
                lines = pl.ds(start, chunk)
                value = sum_ref[row, lines, g.cols(slot)] + term_of(ins, side, i, j, start)
                done[n, lines, :] = (value * gate).astype(BF16)

            if chunk == width:
                some(0)
            else:
                pl.loop(0, width, step=chunk)(some)
            stores.append(pltpu.make_async_copy(done.at[n], out_ref.at[row, :, g.cols(slot)], sems.at[n]))
            stores[-1].start()
        for store in stores:
            store.wait()

    return call(
        kernel,
        [pltpu.VMEM] * (2 + nops) + [pltpu.HBM],
        [(jax.ShapeDtypeStruct(out.shape, out.dtype), pltpu.HBM)],
        [
            pltpu.VMEM((nt, width, width), BF16),
            pltpu.SemaphoreType.DMA((nt,)),
        ],
        (gates, sums, *operands, out),
        aliases={2 + nops: 0},
        flops=flops,
        name=name,
    )[0]


def with_halo(g, link, targets, lists, gates, own, sums, halos, out, name):
    where = {b: (p, n) for p, part in enumerate(lists) for n, b in enumerate(part)}

    def inner(i, j):
        return [k for k in g.inner(i, j, -g.reach, -1) if (k, j) in where]

    def term_of(ins, side, i, j, start):
        total = None
        for k in inner(i, j):
            p, n = where[k, j]
            total = add(total, dot(ins[0][g.row(side, i), :, g.cols(g.slot(side, i, k))], ins[1 + p][n]))
        return total

    flops = 2 * sum(len(inner(i, j)) for i, j in targets) * g.width**3
    return finish(g, link, targets, gates, sums, out, term_of, (own, *halos), flops, name, g.width)


def with_partials(g, link, gates, sums, coded, out):
    width, targets = g.width, g.last_targets

    chunk = width

    def term_of(ins, side, i, j, start):
        n = targets.index((i, j))
        lines = pl.ds(pl.multiple_of(n * width + start, chunk), chunk)
        code = ins[0][lines, :].astype(jnp.int32).astype(F32)
        power = ins[0][pl.ds(len(targets) * width, CODE_ROWS), :].astype(jnp.int32).astype(F32)[n : n + 1]
        return code * jnp.exp2(power - CODE_BITS)

    return finish(g, link, targets, gates, sums, out, term_of, (coded,), 0, "last", chunk)


def on_device(density, block_mask):
    rows, width, strip = density.shape
    g = Band(rows, width, block_mask.shape[1])
    mask = block_mask
    near_blocks = g.first + g.second + g.rest

    first = exchange(pack(g, FAR, g.first, mask, density), FAR)
    packed_second = pack(g, FAR, g.second, mask, density)
    second = exchange(packed_second, FAR)
    later, _ = lax.optimization_barrier((mask, packed_second))
    out, own, sums, near, gates = local(g, near_blocks, later, density)
    near = exchange(near, NEAR)
    coded = exchange(partials(g, FAR, own, first), FAR)
    out = with_halo(g, FAR, g.first_targets, [g.first], gates, own, sums, [first], out, "corner")
    out = with_halo(g, NEAR, g.targets, [near_blocks], gates, own, sums, [near], out, "near")
    out = with_halo(g, FAR, g.second_targets, [g.first, g.second], gates, own, sums, [first, second], out, "edge")
    return with_partials(g, FAR, gates, sums, coded, out)


def solution(mesh):
    in_specs = (P(("groups", "grid"), None, None), P(("groups", "grid"), None))
    out_specs = P(("groups", "grid"), None, None)
    return jax.shard_map(on_device, mesh=mesh, in_specs=in_specs, out_specs=out_specs, check_vma=False)
```

```python
import jax
import jax.numpy as jnp
from jax import lax
from jax.experimental import pallas as pl
from jax.experimental.pallas import tpu as pltpu
from jax.sharding import PartitionSpec as P

F32 = jnp.float32
BF16 = jnp.bfloat16
VMEM_BYTES = 26 * 1024 * 1024
CODE_BITS = 15
WEIGHT = 150
CODE_ROWS = 16
FAR, NEAR = 0, 1


def neighbour_side(link):
    odd = lax.rem(lax.axis_index("grid"), 2)
    return odd if link == FAR else 1 - odd


def exchange(x, link):
    count = lax.axis_size("grid")
    step = [1 if (i % 2 == 0) == (link == NEAR) else -1 for i in range(count)]
    return lax.ppermute(x, "grid", [(i, (i + step[i]) % count) for i in range(count)])


class Band:
    def __init__(self, rows, width, band):
        self.rows = rows
        self.width = width
        self.band = band
        self.reach = reach = (band - 1) // 2
        corner = [(k, j) for k in range(-1, -reach - 1, -1) for j in range(0, k + reach + 1)]
        self.first = [b for b in corner if b[0] > -reach]
        self.opening, self.following = self.first[:2], self.first[2:]
        self.second = [b for b in corner if b[0] == -reach] + [(k, -1) for k in range(-1, -reach - 1, -1)]
        self.rest = [(k, j) for j in range(-2, -reach - 1, -1) for k in range(-1, -reach - 1, -1)]
        self.targets = [(i, j) for i in range(reach) for j in range(i - reach, reach)]
        self.last_targets = [t for t in self.targets if t[1] < -1]
        self.second_targets = [t for t in self.targets if t[1] == -1 or t == (0, 0)]
        self.first_targets = [t for t in self.targets if t[1] >= 0 and t != (0, 0)]

    def row(self, side, i):
        return i + side * (self.rows - 1 - 2 * i)

    def slot(self, side, i, j):
        return self.reach + (1 - 2 * side) * (j - i)

    def cols(self, slot, count=1):
        start = slot * self.width
        return pl.ds(start if isinstance(start, int) else pl.multiple_of(start, self.width), count * self.width)

    def sent(self, side, block):
        k, j = block
        return (1 - side) * (k + self.rows) + side * (-1 - k), self.slot(side, k, j)

    def inner(self, i, j, low, high):
        return range(max(low, i - self.reach, j - self.reach), min(high, i + self.reach, j + self.reach) + 1)


def dot(a, b):
    return jnp.dot(a, b, preferred_element_type=F32)


def add(total, part):
    return part if total is None else total + part


def spec(space):
    return pl.BlockSpec(memory_space=space)


def in_hbm(x):
    return pltpu.with_memory_space_constraint(x, pltpu.HBM)


def call(kernel, ins, outs, scratch, args, aliases=None, flops=0, name=None):
    moved = sum(a.size * a.dtype.itemsize for a in args) + sum(o.size * o.dtype.itemsize for o, _ in outs)
    return pl.pallas_call(
        kernel,
        out_shape=[o for o, _ in outs],
        in_specs=[spec(space) for space in ins],
        out_specs=[spec(space) for _, space in outs],
        scratch_shapes=scratch,
        input_output_aliases=aliases or {},
        compiler_params=pltpu.CompilerParams(vmem_limit_bytes=VMEM_BYTES),
        cost_estimate=pl.CostEstimate(flops=flops, bytes_accessed=moved, transcendentals=0),
        name=name,
    )(*args)


def pack(g, link, blocks, mask, density):
    width = g.width

    def kernel(mask_ref, density_ref, out, marks, mark_sem, sems):
        theirs = 1 - neighbour_side(link)
        mark = pltpu.make_async_copy(mask_ref, marks, mark_sem)
        mark.start()
        copies = []
        for n, block in enumerate(blocks):
            row, slot = g.sent(theirs, block)
            copies.append(pltpu.make_async_copy(density_ref.at[row, :, g.cols(slot)], out.at[n], sems.at[n]))
            copies[-1].start()
        mark.wait()
        for n, block in enumerate(blocks):
            copies[n].wait()
            row, slot = g.sent(theirs, block)

            @pl.when(marks[row, slot] == 0)
            def _():
                out[n] = jnp.zeros((width, width), BF16)

    return call(
        kernel,
        [pltpu.HBM, pltpu.HBM],
        [(jax.ShapeDtypeStruct((len(blocks), width, width), BF16), pltpu.VMEM)],
        [
            pltpu.SMEM(mask.shape, jnp.int32),
            pltpu.SemaphoreType.DMA,
            pltpu.SemaphoreType.DMA((len(blocks),)),
        ],
        (in_hbm(mask), in_hbm(density)),
        name="pack",
    )[0]


def local(g, near_blocks, mask, density):
    rows, width, strip = density.shape
    reach, band = g.reach, g.band

    def kernel(mask_ref, density_ref, out_ref, own, sums, near, gates, done, in_sems, out_sems, near_sems):
        loads = [pltpu.make_async_copy(density_ref.at[r], own.at[r], in_sems.at[r]) for r in range(rows)]
        for load in loads:
            load.start()
        for r in range(rows):
            loads[r].wait()
            for s in range(band):

                @pl.when(mask_ref[r, s] == 0)
                def _():
                    own[r, :, g.cols(s)] = jnp.zeros((width, width), BF16)

                gates[r * band + s] = jnp.full((1, width), mask_ref[r, s].astype(F32))

        stores = []
        for n, block in enumerate(near_blocks):
            row, slot = g.sent(1 - neighbour_side(NEAR), block)
            stores.append(pltpu.make_async_copy(own.at[row, :, g.cols(slot)], near.at[n], near_sems.at[n]))
            stores[-1].start()
        for i in range(rows):
            side = 0 if 2 * i < rows else 1
            final = max(0, band - 2 * reach + g.row(side, i))
            for s in range(band):
                j = i + s - reach
                total = None
                for k in g.inner(i, j, 0, rows - 1):
                    total = add(total, dot(own[i, :, g.cols(k - i + reach)], own[k, :, g.cols(j - k + reach)]))
                ends = s >= band - final if side == 0 else s < final
                if ends:
                    done[i, :, g.cols(s)] = jnp.where(mask_ref[i, s] == 0, 0.0, total).astype(BF16)
                else:
                    sums[i, :, g.cols(s)] = total
            give = g.cols(band - final, final) if side == 0 else g.cols(0, final)
            stores.append(pltpu.make_async_copy(done.at[i, :, give], out_ref.at[i, :, give], out_sems.at[i]))
            stores[-1].start()
        for store in stores:
            store.wait()

    return call(
        kernel,
        [pltpu.SMEM, pltpu.HBM],
        [
            (jax.ShapeDtypeStruct(density.shape, BF16), pltpu.HBM),
            (jax.ShapeDtypeStruct(density.shape, BF16), pltpu.VMEM),
            (jax.ShapeDtypeStruct(density.shape, F32), pltpu.VMEM),
            (jax.ShapeDtypeStruct((len(near_blocks), width, width), BF16), pltpu.VMEM),
            (jax.ShapeDtypeStruct((rows * band, 1, width), F32), pltpu.VMEM),
        ],
        [
            pltpu.VMEM(density.shape, BF16),
            pltpu.SemaphoreType.DMA((rows,)),
            pltpu.SemaphoreType.DMA((rows,)),
            pltpu.SemaphoreType.DMA((len(near_blocks),)),
        ],
        (mask, in_hbm(density)),
        flops=2 * 160 * width**3,
        name="local",
    )


def partials(g, link, own, lists, halos):
    width, reach = g.width, g.reach
    targets = g.last_targets
    where = {b: (p, n) for p, part in enumerate(lists) for n, b in enumerate(part)}

    def kernel(own_ref, *refs):
        out = refs[-1]
        theirs = 1 - neighbour_side(link)
        row_ids = lax.broadcasted_iota(jnp.int32, (CODE_ROWS, width), 0)
        powers = jnp.zeros((CODE_ROWS, width), F32)
        for n, (i, j) in enumerate(targets):
            total = None
            for k in g.inner(i, j, -reach, -1):
                row, slot = g.sent(theirs, (k, j))
                p, m = where[-1 - i, -1 - k]
                total = add(total, dot(refs[p][m], own_ref[row, :, g.cols(slot)]))
            top = jnp.maximum(jnp.max(jnp.abs(total), axis=0, keepdims=True), 2.0**-110)
            power = jnp.ceil(jnp.log2(top) + 0.001)
            code = jnp.round(total * jnp.exp2(CODE_BITS - power))
            out[pl.ds(n * width, width), :] = code.astype(jnp.int32).astype(jnp.int16)
            powers = jnp.where(row_ids == n, power, powers)
        out[pl.ds(len(targets) * width, CODE_ROWS), :] = powers.astype(jnp.int32).astype(jnp.int16)

    return call(
        kernel,
        [pltpu.VMEM] * (1 + len(halos)),
        [(jax.ShapeDtypeStruct((len(targets) * width + CODE_ROWS, width), jnp.int16), pltpu.VMEM)],
        [],
        (own, *halos),
        flops=WEIGHT * 2 * 8 * width**3,
        name="partials",
    )[0]


def finish(g, link, targets, gates, sums, out, term_of, operands, flops, name, chunk):
    width = g.width
    nt, nops = len(targets), len(operands)

    def kernel(gate_ref, sum_ref, *refs):
        ins, (out_ref, done, sems) = refs[:nops], refs[nops + 1 :]
        side = neighbour_side(link)
        stores = []
        for n, (i, j) in enumerate(targets):
            row, slot = g.row(side, i), g.slot(side, i, j)
            gate = gate_ref[row * g.band + slot]

            def some(start):
                lines = pl.ds(start, chunk)
                value = sum_ref[row, lines, g.cols(slot)] + term_of(ins, side, i, j, start)
                done[n, lines, :] = (value * gate).astype(BF16)

            if chunk == width:
                some(0)
            else:
                pl.loop(0, width, step=chunk)(some)
            stores.append(pltpu.make_async_copy(done.at[n], out_ref.at[row, :, g.cols(slot)], sems.at[n]))
            stores[-1].start()
        for store in stores:
            store.wait()

    return call(
        kernel,
        [pltpu.VMEM] * (2 + nops) + [pltpu.HBM],
        [(jax.ShapeDtypeStruct(out.shape, out.dtype), pltpu.HBM)],
        [
            pltpu.VMEM((nt, width, width), BF16),
            pltpu.SemaphoreType.DMA((nt,)),
        ],
        (gates, sums, *operands, out),
        aliases={2 + nops: 0},
        flops=flops,
        name=name,
    )[0]


def with_halo(g, link, targets, lists, gates, own, sums, halos, out, name):
    where = {b: (p, n) for p, part in enumerate(lists) for n, b in enumerate(part)}

    def inner(i, j):
        return [k for k in g.inner(i, j, -g.reach, -1) if (k, j) in where]

    def term_of(ins, side, i, j, start):
        total = None
        for k in inner(i, j):
            p, n = where[k, j]
            total = add(total, dot(ins[0][g.row(side, i), :, g.cols(g.slot(side, i, k))], ins[1 + p][n]))
        return total

    flops = 2 * sum(len(inner(i, j)) for i, j in targets) * g.width**3
    return finish(g, link, targets, gates, sums, out, term_of, (own, *halos), flops, name, g.width)


def with_partials(g, link, gates, sums, coded, out):
    width, targets = g.width, g.last_targets

    chunk = width

    def term_of(ins, side, i, j, start):
        n = targets.index((i, j))
        lines = pl.ds(pl.multiple_of(n * width + start, chunk), chunk)
        code = ins[0][lines, :].astype(jnp.int32).astype(F32)
        power = ins[0][pl.ds(len(targets) * width, CODE_ROWS), :].astype(jnp.int32).astype(F32)[n : n + 1]
        return code * jnp.exp2(power - CODE_BITS)

    return finish(g, link, targets, gates, sums, out, term_of, (coded,), 0, "last", chunk)


def on_device(density, block_mask):
    rows, width, strip = density.shape
    g = Band(rows, width, block_mask.shape[1])
    mask = block_mask
    near_blocks = g.first + g.second + g.rest

    packed_opening = pack(g, FAR, g.opening, mask, density)
    opening = exchange(packed_opening, FAR)
    later, _ = lax.optimization_barrier((mask, packed_opening))
    packed_following = pack(g, FAR, g.following, later, density)
    following = exchange(packed_following, FAR)
    later, _ = lax.optimization_barrier((mask, packed_following))
    packed_second = pack(g, FAR, g.second, later, density)
    second = exchange(packed_second, FAR)
    later, _ = lax.optimization_barrier((mask, packed_second))
    out, own, sums, near, gates = local(g, near_blocks, later, density)
    near = exchange(near, NEAR)

    lists, halos = [g.opening, g.following], [opening, following]
    coded = exchange(partials(g, FAR, own, lists, halos), FAR)
    out = with_halo(g, FAR, g.first_targets, lists, gates, own, sums, halos, out, "corner")
    out = with_halo(g, NEAR, g.targets, [near_blocks], gates, own, sums, [near], out, "near")
    lists, halos = lists + [g.second], halos + [second]
    out = with_halo(g, FAR, g.second_targets, lists, gates, own, sums, halos, out, "edge")
    return with_partials(g, FAR, gates, sums, coded, out)


def solution(mesh):
    in_specs = (P(("groups", "grid"), None, None), P(("groups", "grid"), None))
    out_specs = P(("groups", "grid"), None, None)
    return jax.shard_map(on_device, mesh=mesh, in_specs=in_specs, out_specs=out_specs, check_vma=False)
```

```python
import jax
import jax.numpy as jnp
from jax import lax
from jax.experimental import pallas as pl
from jax.experimental.pallas import tpu as pltpu
from jax.sharding import PartitionSpec as P

F32 = jnp.float32
BF16 = jnp.bfloat16
VMEM_BYTES = 26 * 1024 * 1024
CODE_BITS = 15
WEIGHT = 150
CODE_ROWS = 16
LANES = 128
FAR, NEAR = 0, 1


def neighbour_side(link):
    odd = lax.rem(lax.axis_index("grid"), 2)
    return odd if link == FAR else 1 - odd


def exchange(x, link):
    count = lax.axis_size("grid")
    step = [1 if (i % 2 == 0) == (link == NEAR) else -1 for i in range(count)]
    return lax.ppermute(x, "grid", [(i, (i + step[i]) % count) for i in range(count)])


class Band:
    def __init__(self, rows, width, band):
        self.rows = rows
        self.width = width
        self.band = band
        self.reach = reach = (band - 1) // 2
        corner = [(k, j) for k in range(-1, -reach - 1, -1) for j in range(0, k + reach + 1)]
        self.first = [b for b in corner if b[0] > -reach]
        self.opening, self.following = self.first[:2], self.first[2:]
        self.second = [b for b in corner if b[0] == -reach] + [(k, -1) for k in range(-1, -reach - 1, -1)]
        self.rest = [(k, j) for j in range(-2, -reach - 1, -1) for k in range(-1, -reach - 1, -1)]
        self.targets = [(i, j) for i in range(reach) for j in range(i - reach, reach)]
        self.last_targets = [t for t in self.targets if t[1] < -1]
        self.early_targets, self.final_targets = self.last_targets[:-1], self.last_targets[-1:]
        self.second_targets = [t for t in self.targets if t[1] == -1 or t == (0, 0)]
        self.first_targets = [t for t in self.targets if t[1] >= 0 and t != (0, 0)]

    def row(self, side, i):
        return i + side * (self.rows - 1 - 2 * i)

    def slot(self, side, i, j):
        return self.reach + (1 - 2 * side) * (j - i)

    def cols(self, slot, count=1):
        start = slot * self.width
        return pl.ds(start if isinstance(start, int) else pl.multiple_of(start, self.width), count * self.width)

    def sent(self, side, block):
        k, j = block
        return (1 - side) * (k + self.rows) + side * (-1 - k), self.slot(side, k, j)

    def inner(self, i, j, low, high):
        return range(max(low, i - self.reach, j - self.reach), min(high, i + self.reach, j + self.reach) + 1)


def dot(a, b):
    return jnp.dot(a, b, preferred_element_type=F32)


def add(total, part):
    return part if total is None else total + part


def spec(space):
    return pl.BlockSpec(memory_space=space)


def in_hbm(x):
    return pltpu.with_memory_space_constraint(x, pltpu.HBM)


def call(kernel, ins, outs, scratch, args, aliases=None, flops=0, name=None):
    moved = sum(a.size * a.dtype.itemsize for a in args) + sum(o.size * o.dtype.itemsize for o, _ in outs)
    return pl.pallas_call(
        kernel,
        out_shape=[o for o, _ in outs],
        in_specs=[spec(space) for space in ins],
        out_specs=[spec(space) for _, space in outs],
        scratch_shapes=scratch,
        input_output_aliases=aliases or {},
        compiler_params=pltpu.CompilerParams(vmem_limit_bytes=VMEM_BYTES),
        cost_estimate=pl.CostEstimate(flops=flops, bytes_accessed=moved, transcendentals=0),
        name=name,
    )(*args)


def pack(g, link, blocks, mask, density):
    width = g.width

    def kernel(mask_ref, density_ref, out, marks, mark_sem, sems):
        theirs = 1 - neighbour_side(link)
        mark = pltpu.make_async_copy(mask_ref, marks, mark_sem)
        mark.start()
        copies = []
        for n, block in enumerate(blocks):
            row, slot = g.sent(theirs, block)
            copies.append(pltpu.make_async_copy(density_ref.at[row, :, g.cols(slot)], out.at[n], sems.at[n]))
            copies[-1].start()
        mark.wait()
        for n, block in enumerate(blocks):
            copies[n].wait()
            row, slot = g.sent(theirs, block)

            @pl.when(marks[row, slot] == 0)
            def _():
                out[n] = jnp.zeros((width, width), BF16)

    return call(
        kernel,
        [pltpu.HBM, pltpu.HBM],
        [(jax.ShapeDtypeStruct((len(blocks), width, width), BF16), pltpu.VMEM)],
        [
            pltpu.SMEM(mask.shape, jnp.int32),
            pltpu.SemaphoreType.DMA,
            pltpu.SemaphoreType.DMA((len(blocks),)),
        ],
        (in_hbm(mask), in_hbm(density)),
        name="pack",
    )[0]


def local(g, near_blocks, mask, density):
    rows, width, strip = density.shape
    reach, band = g.reach, g.band

    def kernel(mask_ref, density_ref, out_ref, own, sums, near, gates, done, in_sems, out_sems, near_sems):
        loads = [pltpu.make_async_copy(density_ref.at[r], own.at[r], in_sems.at[r]) for r in range(rows)]
        for load in loads:
            load.start()
        for r in range(rows):
            loads[r].wait()
            for s in range(band):

                @pl.when(mask_ref[r, s] == 0)
                def _():
                    own[r, :, g.cols(s)] = jnp.zeros((width, width), BF16)

                gates[r * band + s] = jnp.full((1, width), mask_ref[r, s].astype(F32))

        stores = []
        for n, block in enumerate(near_blocks):
            row, slot = g.sent(1 - neighbour_side(NEAR), block)
            stores.append(pltpu.make_async_copy(own.at[row, :, g.cols(slot)], near.at[n], near_sems.at[n]))
            stores[-1].start()
        for i in range(rows):
            side = 0 if 2 * i < rows else 1
            final = max(0, band - 2 * reach + g.row(side, i))
            for s in range(band):
                j = i + s - reach
                total = None
                for k in g.inner(i, j, 0, rows - 1):
                    total = add(total, dot(own[i, :, g.cols(k - i + reach)], own[k, :, g.cols(j - k + reach)]))
                ends = s >= band - final if side == 0 else s < final
                if ends:
                    done[i, :, g.cols(s)] = jnp.where(mask_ref[i, s] == 0, 0.0, total).astype(BF16)
                else:
                    sums[i, :, g.cols(s)] = total
            give = g.cols(band - final, final) if side == 0 else g.cols(0, final)
            stores.append(pltpu.make_async_copy(done.at[i, :, give], out_ref.at[i, :, give], out_sems.at[i]))
            stores[-1].start()
        for store in stores:
            store.wait()

    return call(
        kernel,
        [pltpu.SMEM, pltpu.HBM],
        [
            (jax.ShapeDtypeStruct(density.shape, BF16), pltpu.HBM),
            (jax.ShapeDtypeStruct(density.shape, BF16), pltpu.VMEM),
            (jax.ShapeDtypeStruct(density.shape, F32), pltpu.VMEM),
            (jax.ShapeDtypeStruct((len(near_blocks), width, width), BF16), pltpu.VMEM),
            (jax.ShapeDtypeStruct((rows * band, 1, width), F32), pltpu.VMEM),
        ],
        [
            pltpu.VMEM(density.shape, BF16),
            pltpu.SemaphoreType.DMA((rows,)),
            pltpu.SemaphoreType.DMA((rows,)),
            pltpu.SemaphoreType.DMA((len(near_blocks),)),
        ],
        (mask, in_hbm(density)),
        flops=2 * 160 * width**3,
        name="local",
    )


def partials(g, link, own, lists, halos):
    width, reach = g.width, g.reach
    strips = width // LANES
    groups = [g.early_targets, g.final_targets]
    where = {b: (p, n) for p, part in enumerate(lists) for n, b in enumerate(part)}

    def kernel(own_ref, *refs):
        outs = refs[-2:]
        theirs = 1 - neighbour_side(link)
        row_ids = lax.broadcasted_iota(jnp.int32, (CODE_ROWS, LANES), 0)
        powers = jnp.zeros((CODE_ROWS, LANES), F32)
        line = 0
        for out, targets in zip(outs, groups):
            for n, (i, j) in enumerate(targets):
                total = None
                for k in g.inner(i, j, -reach, -1):
                    row, slot = g.sent(theirs, (k, j))
                    p, m = where[-1 - i, -1 - k]
                    total = add(total, dot(refs[p][m], own_ref[row, :, g.cols(slot)]))
                top = jnp.maximum(jnp.max(jnp.abs(total), axis=0, keepdims=True), 2.0**-110)
                power = jnp.ceil(jnp.log2(top) + 0.001)
                code = jnp.round(total * jnp.exp2(CODE_BITS - power)).astype(jnp.int32).astype(jnp.int16)
                for h in range(strips):
                    lanes = slice(h * LANES, (h + 1) * LANES)
                    out[pl.ds((n * strips + h) * width, width), :] = code[:, lanes]
                    powers = jnp.where(row_ids == line, power[:, lanes], powers)
                    line += 1
        outs[0][pl.ds(len(groups[0]) * strips * width, CODE_ROWS), :] = powers.astype(jnp.int32).astype(jnp.int16)

    def result(lines):
        return jax.ShapeDtypeStruct((lines, LANES), jnp.int16), pltpu.VMEM

    return call(
        kernel,
        [pltpu.VMEM] * (1 + len(halos)),
        [result(len(groups[0]) * strips * width + CODE_ROWS), result(len(groups[1]) * strips * width)],
        [],
        (own, *halos),
        flops=WEIGHT * 2 * 8 * width**3,
        name="partials",
    )


def finish(g, link, targets, gates, sums, out, term_of, operands, flops, name):
    width = g.width
    nt, nops = len(targets), len(operands)

    def kernel(gate_ref, sum_ref, *refs):
        ins, (out_ref, done, sems) = refs[:nops], refs[nops + 1 :]
        side = neighbour_side(link)
        stores = []
        for n, (i, j) in enumerate(targets):
            row, slot = g.row(side, i), g.slot(side, i, j)
            value = sum_ref[row, :, g.cols(slot)] + term_of(ins, side, i, j)
            done[n] = (value * gate_ref[row * g.band + slot]).astype(BF16)
            stores.append(pltpu.make_async_copy(done.at[n], out_ref.at[row, :, g.cols(slot)], sems.at[n]))
            stores[-1].start()
        for store in stores:
            store.wait()

    return call(
        kernel,
        [pltpu.VMEM] * (2 + nops) + [pltpu.HBM],
        [(jax.ShapeDtypeStruct(out.shape, out.dtype), pltpu.HBM)],
        [
            pltpu.VMEM((nt, width, width), BF16),
            pltpu.SemaphoreType.DMA((nt,)),
        ],
        (gates, sums, *operands, out),
        aliases={2 + nops: 0},
        flops=flops,
        name=name,
    )[0]


def with_halo(g, link, targets, lists, gates, own, sums, halos, out, name):
    where = {b: (p, n) for p, part in enumerate(lists) for n, b in enumerate(part)}

    def inner(i, j):
        return [k for k in g.inner(i, j, -g.reach, -1) if (k, j) in where]

    def term_of(ins, side, i, j):
        total = None
        for k in inner(i, j):
            p, n = where[k, j]
            total = add(total, dot(ins[0][g.row(side, i), :, g.cols(g.slot(side, i, k))], ins[1 + p][n]))
        return total

    flops = 2 * sum(len(inner(i, j)) for i, j in targets) * g.width**3
    return finish(g, link, targets, gates, sums, out, term_of, (own, *halos), flops, name)


def with_partials(g, link, targets, gates, sums, coded, out, name):
    width = g.width
    strips = width // LANES
    powers_at = len(g.early_targets) * strips * width

    def term_of(ins, side, i, j):
        n, line = targets.index((i, j)), g.last_targets.index((i, j)) * strips
        powers = ins[0][pl.ds(powers_at, CODE_ROWS), :].astype(jnp.int32).astype(F32)
        parts = []
        for h in range(strips):
            code = ins[-1][pl.ds((n * strips + h) * width, width), :].astype(jnp.int32).astype(F32)
            parts.append(code * jnp.exp2(powers[line + h : line + h + 1] - CODE_BITS))
        return jnp.concatenate(parts, axis=1)

    return finish(g, link, targets, gates, sums, out, term_of, coded, 0, name)


def on_device(density, block_mask):
    rows, width, strip = density.shape
    g = Band(rows, width, block_mask.shape[1])
    mask = block_mask
    near_blocks = g.first + g.second + g.rest

    packed_opening = pack(g, FAR, g.opening, mask, density)
    opening = exchange(packed_opening, FAR)
    later, _ = lax.optimization_barrier((mask, packed_opening))
    packed_following = pack(g, FAR, g.following, later, density)
    following = exchange(packed_following, FAR)
    later, _ = lax.optimization_barrier((mask, packed_following))
    packed_second = pack(g, FAR, g.second, later, density)
    second = exchange(packed_second, FAR)
    later, _ = lax.optimization_barrier((mask, packed_second))
    out, own, sums, near, gates = local(g, near_blocks, later, density)
    near = exchange(near, NEAR)

    lists, halos = [g.opening, g.following], [opening, following]
    early, final = partials(g, FAR, own, lists, halos)
    early = exchange(early, FAR)
    final = exchange(final, FAR)
    out = with_halo(g, FAR, g.first_targets, lists, gates, own, sums, halos, out, "corner")
    out = with_halo(g, NEAR, g.targets, [near_blocks], gates, own, sums, [near], out, "near")
    lists, halos = lists + [g.second], halos + [second]
    out = with_halo(g, FAR, g.second_targets, lists, gates, own, sums, halos, out, "edge")
    out = with_partials(g, FAR, g.early_targets, gates, sums, (early,), out, "early")
    return with_partials(g, FAR, g.final_targets, gates, sums, (early, final), out, "final")


def solution(mesh):
    in_specs = (P(("groups", "grid"), None, None), P(("groups", "grid"), None))
    out_specs = P(("groups", "grid"), None, None)
    return jax.shard_map(on_device, mesh=mesh, in_specs=in_specs, out_specs=out_specs, check_vma=False)
```

```python
import jax
import jax.numpy as jnp
from jax import lax
from jax.experimental import pallas as pl
from jax.experimental.pallas import tpu as pltpu
from jax.sharding import PartitionSpec as P

F32 = jnp.float32
BF16 = jnp.bfloat16
VMEM_BYTES = 26 * 1024 * 1024
CODE_BITS = 15
WEIGHT = 150
CODE_ROWS = 16
LANES = 128
FAR, NEAR = 0, 1


def neighbour_side(link):
    odd = lax.rem(lax.axis_index("grid"), 2)
    return odd if link == FAR else 1 - odd


def exchange(x, link):
    count = lax.axis_size("grid")
    step = [1 if (i % 2 == 0) == (link == NEAR) else -1 for i in range(count)]
    return lax.ppermute(x, "grid", [(i, (i + step[i]) % count) for i in range(count)])


class Band:
    def __init__(self, rows, width, band):
        self.rows = rows
        self.width = width
        self.band = band
        self.reach = reach = (band - 1) // 2
        corner = [(k, j) for k in range(-1, -reach - 1, -1) for j in range(0, k + reach + 1)]
        self.first = [b for b in corner if b[0] > -reach]
        self.opening, self.following = self.first[:2], self.first[2:]
        self.second = [b for b in corner if b[0] == -reach] + [(k, -1) for k in range(-1, -reach - 1, -1)]
        self.rest = [(k, j) for j in range(-2, -reach - 1, -1) for k in range(-1, -reach - 1, -1)]
        self.targets = [(i, j) for i in range(reach) for j in range(i - reach, reach)]
        self.last_targets = [t for t in self.targets if t[1] < -1]
        self.early_targets, self.final_targets = self.last_targets[:-1], self.last_targets[-1:]
        self.second_targets = [t for t in self.targets if t[1] == -1 or t == (0, 0)]
        self.first_targets = [t for t in self.targets if t[1] >= 0 and t != (0, 0)]

    def row(self, side, i):
        return i + side * (self.rows - 1 - 2 * i)

    def slot(self, side, i, j):
        return self.reach + (1 - 2 * side) * (j - i)

    def cols(self, slot, count=1):
        start = slot * self.width
        return pl.ds(start if isinstance(start, int) else pl.multiple_of(start, self.width), count * self.width)

    def sent(self, side, block):
        k, j = block
        return (1 - side) * (k + self.rows) + side * (-1 - k), self.slot(side, k, j)

    def inner(self, i, j, low, high):
        return range(max(low, i - self.reach, j - self.reach), min(high, i + self.reach, j + self.reach) + 1)


def dot(a, b):
    return jnp.dot(a, b, preferred_element_type=F32)


def add(total, part):
    return part if total is None else total + part


def spec(space):
    return pl.BlockSpec(memory_space=space)


def in_hbm(x):
    return pltpu.with_memory_space_constraint(x, pltpu.HBM)


def call(kernel, ins, outs, scratch, args, aliases=None, flops=0, name=None):
    moved = sum(a.size * a.dtype.itemsize for a in args) + sum(o.size * o.dtype.itemsize for o, _ in outs)
    return pl.pallas_call(
        kernel,
        out_shape=[o for o, _ in outs],
        in_specs=[spec(space) for space in ins],
        out_specs=[spec(space) for _, space in outs],
        scratch_shapes=scratch,
        input_output_aliases=aliases or {},
        compiler_params=pltpu.CompilerParams(vmem_limit_bytes=VMEM_BYTES),
        cost_estimate=pl.CostEstimate(flops=flops, bytes_accessed=moved, transcendentals=0),
        name=name,
    )(*args)


def pack(g, link, blocks, mask, density):
    width = g.width

    def kernel(mask_ref, density_ref, out, marks, mark_sem, sems):
        theirs = 1 - neighbour_side(link)
        mark = pltpu.make_async_copy(mask_ref, marks, mark_sem)
        mark.start()
        copies = []
        for n, block in enumerate(blocks):
            row, slot = g.sent(theirs, block)
            copies.append(pltpu.make_async_copy(density_ref.at[row, :, g.cols(slot)], out.at[n], sems.at[n]))
            copies[-1].start()
        mark.wait()
        for n, block in enumerate(blocks):
            copies[n].wait()
            row, slot = g.sent(theirs, block)

            @pl.when(marks[row, slot] == 0)
            def _():
                out[n] = jnp.zeros((width, width), BF16)

    return call(
        kernel,
        [pltpu.HBM, pltpu.HBM],
        [(jax.ShapeDtypeStruct((len(blocks), width, width), BF16), pltpu.VMEM)],
        [
            pltpu.SMEM(mask.shape, jnp.int32),
            pltpu.SemaphoreType.DMA,
            pltpu.SemaphoreType.DMA((len(blocks),)),
        ],
        (in_hbm(mask), in_hbm(density)),
        name="pack",
    )[0]


def local(g, near_blocks, mask, density):
    rows, width, strip = density.shape
    reach, band = g.reach, g.band

    def kernel(mask_ref, density_ref, out_ref, own, sums, near, gates, done, in_sems, out_sems, near_sems):
        loads = [pltpu.make_async_copy(density_ref.at[r], own.at[r], in_sems.at[r]) for r in range(rows)]
        for load in loads:
            load.start()
        for r in range(rows):
            loads[r].wait()
            for s in range(band):

                @pl.when(mask_ref[r, s] == 0)
                def _():
                    own[r, :, g.cols(s)] = jnp.zeros((width, width), BF16)

                gates[r * band + s] = jnp.full((1, width), mask_ref[r, s].astype(F32))

        stores = []
        for n, block in enumerate(near_blocks):
            row, slot = g.sent(1 - neighbour_side(NEAR), block)
            stores.append(pltpu.make_async_copy(own.at[row, :, g.cols(slot)], near.at[n], near_sems.at[n]))
            stores[-1].start()
        for i in range(rows):
            side = 0 if 2 * i < rows else 1
            final = max(0, band - 2 * reach + g.row(side, i))
            for s in range(band):
                j = i + s - reach
                total = None
                for k in g.inner(i, j, 0, rows - 1):
                    total = add(total, dot(own[i, :, g.cols(k - i + reach)], own[k, :, g.cols(j - k + reach)]))
                ends = s >= band - final if side == 0 else s < final
                if ends:
                    done[i, :, g.cols(s)] = jnp.where(mask_ref[i, s] == 0, 0.0, total).astype(BF16)
                else:
                    sums[i, :, g.cols(s)] = total
            give = g.cols(band - final, final) if side == 0 else g.cols(0, final)
            stores.append(pltpu.make_async_copy(done.at[i, :, give], out_ref.at[i, :, give], out_sems.at[i]))
            stores[-1].start()
        for store in stores:
            store.wait()

    return call(
        kernel,
        [pltpu.SMEM, pltpu.HBM],
        [
            (jax.ShapeDtypeStruct(density.shape, BF16), pltpu.HBM),
            (jax.ShapeDtypeStruct(density.shape, BF16), pltpu.VMEM),
            (jax.ShapeDtypeStruct(density.shape, F32), pltpu.VMEM),
            (jax.ShapeDtypeStruct((len(near_blocks), width, width), BF16), pltpu.VMEM),
            (jax.ShapeDtypeStruct((rows * band, 1, width), F32), pltpu.VMEM),
        ],
        [
            pltpu.VMEM(density.shape, BF16),
            pltpu.SemaphoreType.DMA((rows,)),
            pltpu.SemaphoreType.DMA((rows,)),
            pltpu.SemaphoreType.DMA((len(near_blocks),)),
        ],
        (mask, in_hbm(density)),
        flops=2 * 160 * width**3,
        name="local",
    )


def partials(g, link, own, lists, halos):
    width, reach = g.width, g.reach
    strips = width // LANES
    groups = [g.early_targets, g.final_targets]
    where = {b: (p, n) for p, part in enumerate(lists) for n, b in enumerate(part)}

    def kernel(own_ref, *refs):
        outs = refs[-2:]
        theirs = 1 - neighbour_side(link)
        row_ids = lax.broadcasted_iota(jnp.int32, (CODE_ROWS, LANES), 0)
        powers = jnp.zeros((CODE_ROWS, LANES), F32)
        line = 0
        for out, targets in zip(outs, groups):
            for n, (i, j) in enumerate(targets):
                total = None
                for k in g.inner(i, j, -reach, -1):
                    row, slot = g.sent(theirs, (k, j))
                    p, m = where[-1 - i, -1 - k]
                    total = add(total, dot(refs[p][m], own_ref[row, :, g.cols(slot)]))
                top = jnp.maximum(jnp.max(jnp.abs(total), axis=0, keepdims=True), 2.0**-110)
                power = jnp.ceil(jnp.log2(top) + 0.001)
                code = jnp.round(total * jnp.exp2(CODE_BITS - power)).astype(jnp.int32).astype(jnp.int16)
                for h in range(strips):
                    lanes = slice(h * LANES, (h + 1) * LANES)
                    out[pl.ds((n * strips + h) * width, width), :] = code[:, lanes]
                    powers = jnp.where(row_ids == line, power[:, lanes], powers)
                    line += 1
        outs[0][pl.ds(len(groups[0]) * strips * width, CODE_ROWS), :] = powers.astype(jnp.int32).astype(jnp.int16)

    def result(lines):
        return jax.ShapeDtypeStruct((lines, LANES), jnp.int16), pltpu.VMEM

    return call(
        kernel,
        [pltpu.VMEM] * (1 + len(halos)),
        [result(len(groups[0]) * strips * width + CODE_ROWS), result(len(groups[1]) * strips * width)],
        [],
        (own, *halos),
        flops=WEIGHT * 2 * 8 * width**3,
        name="partials",
    )


def finish(g, link, targets, gates, sums, out, term_of, operands, flops, name):
    width = g.width
    nt, nops = len(targets), len(operands)

    def kernel(gate_ref, sum_ref, *refs):
        ins, (out_ref, done, sems) = refs[:nops], refs[nops + 1 :]
        side = neighbour_side(link)
        stores = []
        for n, (i, j) in enumerate(targets):
            row, slot = g.row(side, i), g.slot(side, i, j)
            value = sum_ref[row, :, g.cols(slot)] + term_of(ins, side, i, j)
            done[n] = (value * gate_ref[row * g.band + slot]).astype(BF16)
            stores.append(pltpu.make_async_copy(done.at[n], out_ref.at[row, :, g.cols(slot)], sems.at[n]))
            stores[-1].start()
        for store in stores:
            store.wait()

    return call(
        kernel,
        [pltpu.VMEM] * (2 + nops) + [pltpu.HBM],
        [(jax.ShapeDtypeStruct(out.shape, out.dtype), pltpu.HBM)],
        [
            pltpu.VMEM((nt, width, width), BF16),
            pltpu.SemaphoreType.DMA((nt,)),
        ],
        (gates, sums, *operands, out),
        aliases={2 + nops: 0},
        flops=flops,
        name=name,
    )[0]


def with_halo(g, link, targets, lists, gates, own, sums, halos, out, name):
    where = {b: (p, n) for p, part in enumerate(lists) for n, b in enumerate(part)}

    def inner(i, j):
        return [k for k in g.inner(i, j, -g.reach, -1) if (k, j) in where]

    def term_of(ins, side, i, j):
        total = None
        for k in inner(i, j):
            p, n = where[k, j]
            total = add(total, dot(ins[0][g.row(side, i), :, g.cols(g.slot(side, i, k))], ins[1 + p][n]))
        return total

    flops = 2 * sum(len(inner(i, j)) for i, j in targets) * g.width**3
    return finish(g, link, targets, gates, sums, out, term_of, (own, *halos), flops, name)


def with_partials(g, link, targets, gates, sums, coded, out, name):
    width = g.width
    strips = width // LANES
    powers_at = len(g.early_targets) * strips * width

    def term_of(ins, side, i, j):
        n, line = targets.index((i, j)), g.last_targets.index((i, j)) * strips
        powers = ins[0][pl.ds(powers_at, CODE_ROWS), :].astype(jnp.int32).astype(F32)
        parts = []
        for h in range(strips):
            code = ins[-1][pl.ds((n * strips + h) * width, width), :].astype(jnp.int32).astype(F32)
            parts.append(code * jnp.exp2(powers[line + h : line + h + 1] - CODE_BITS))
        return jnp.concatenate(parts, axis=1)

    return finish(g, link, targets, gates, sums, out, term_of, coded, 0, name)


def on_device(density, block_mask):
    rows, width, strip = density.shape
    g = Band(rows, width, block_mask.shape[1])
    mask = block_mask
    near_blocks = g.first + g.second + g.rest

    packed_opening = pack(g, FAR, g.opening, mask, density)
    opening = exchange(packed_opening, FAR)
    later, _ = lax.optimization_barrier((mask, packed_opening))
    packed_following = pack(g, FAR, g.following, later, density)
    following = exchange(packed_following, FAR)
    later, _ = lax.optimization_barrier((mask, packed_following))
    packed_second = pack(g, FAR, g.second, later, density)
    second = exchange(packed_second, FAR)
    later, _ = lax.optimization_barrier((mask, packed_second))
    out, own, sums, near, gates = local(g, near_blocks, later, density)
    near = exchange(near, NEAR)

    lists, halos = [g.opening, g.following], [opening, following]
    early, final = partials(g, FAR, own, lists, halos)
    early = exchange(early, FAR)
    final = exchange(final, FAR)
    out = with_halo(g, NEAR, g.targets, [near_blocks], gates, own, sums, [near], out, "near")
    lists, halos = lists + [g.second], halos + [second]
    out = with_halo(g, FAR, g.first_targets + g.second_targets, lists, gates, own, sums, halos, out, "edge")
    out = with_partials(g, FAR, g.early_targets, gates, sums, (early,), out, "early")
    return with_partials(g, FAR, g.final_targets, gates, sums, (early, final), out, "final")


def solution(mesh):
    in_specs = (P(("groups", "grid"), None, None), P(("groups", "grid"), None))
    out_specs = P(("groups", "grid"), None, None)
    return jax.shard_map(on_device, mesh=mesh, in_specs=in_specs, out_specs=out_specs, check_vma=False)
```

```python
import jax
import jax.numpy as jnp
from jax import lax
from jax.experimental import pallas as pl
from jax.experimental.pallas import tpu as pltpu
from jax.sharding import PartitionSpec as P

F32 = jnp.float32
BF16 = jnp.bfloat16
VMEM_BYTES = 26 * 1024 * 1024
CODE_BITS = 15
WEIGHT = 150
CODE_ROWS = 16
LANES = 128
PIECES = 4
FAR, NEAR = 0, 1


def neighbour_side(link):
    odd = lax.rem(lax.axis_index("grid"), 2)
    return odd if link == FAR else 1 - odd


def exchange(x, link):
    count = lax.axis_size("grid")
    step = [1 if (i % 2 == 0) == (link == NEAR) else -1 for i in range(count)]
    return lax.ppermute(x, "grid", [(i, (i + step[i]) % count) for i in range(count)])


class Band:
    def __init__(self, rows, width, band):
        self.rows = rows
        self.width = width
        self.band = band
        self.reach = reach = (band - 1) // 2
        corner = [(k, j) for k in range(-1, -reach - 1, -1) for j in range(0, k + reach + 1)]
        self.first = [b for b in corner if b[0] > -reach]
        self.opening, self.following = self.first[:2], self.first[2:]
        self.second = [b for b in corner if b[0] == -reach] + [(k, -1) for k in range(-1, -reach - 1, -1)]
        self.rest = [(k, j) for j in range(-2, -reach - 1, -1) for k in range(-1, -reach - 1, -1)]
        self.targets = [(i, j) for i in range(reach) for j in range(i - reach, reach)]
        self.last_targets = [t for t in self.targets if t[1] < -1]
        self.early_targets, self.final_targets = self.last_targets[:-1], self.last_targets[-1:]
        self.second_targets = [t for t in self.targets if t[1] == -1 or t == (0, 0)]
        self.first_targets = [t for t in self.targets if t[1] >= 0 and t != (0, 0)]

    def row(self, side, i):
        return i + side * (self.rows - 1 - 2 * i)

    def slot(self, side, i, j):
        return self.reach + (1 - 2 * side) * (j - i)

    def cols(self, slot, count=1):
        start = slot * self.width
        return pl.ds(start if isinstance(start, int) else pl.multiple_of(start, self.width), count * self.width)

    def sent(self, side, block):
        k, j = block
        return (1 - side) * (k + self.rows) + side * (-1 - k), self.slot(side, k, j)

    def inner(self, i, j, low, high):
        return range(max(low, i - self.reach, j - self.reach), min(high, i + self.reach, j + self.reach) + 1)


def dot(a, b):
    return jnp.dot(a, b, preferred_element_type=F32)


def add(total, part):
    return part if total is None else total + part


def spec(space):
    return pl.BlockSpec(memory_space=space)


def in_hbm(x):
    return pltpu.with_memory_space_constraint(x, pltpu.HBM)


def call(kernel, ins, outs, scratch, args, aliases=None, flops=0, name=None):
    moved = sum(a.size * a.dtype.itemsize for a in args) + sum(o.size * o.dtype.itemsize for o, _ in outs)
    return pl.pallas_call(
        kernel,
        out_shape=[o for o, _ in outs],
        in_specs=[spec(space) for space in ins],
        out_specs=[spec(space) for _, space in outs],
        scratch_shapes=scratch,
        input_output_aliases=aliases or {},
        compiler_params=pltpu.CompilerParams(vmem_limit_bytes=VMEM_BYTES),
        cost_estimate=pl.CostEstimate(flops=flops, bytes_accessed=moved, transcendentals=0),
        name=name,
    )(*args)


def pack(g, link, blocks, mask, density):
    width = g.width

    def kernel(mask_ref, density_ref, out, marks, mark_sem, sems):
        theirs = 1 - neighbour_side(link)
        mark = pltpu.make_async_copy(mask_ref, marks, mark_sem)
        mark.start()
        copies = []
        for n, block in enumerate(blocks):
            row, slot = g.sent(theirs, block)
            for piece in range(PIECES):
                lines = pl.ds(piece * (width // PIECES), width // PIECES)
                source = density_ref.at[row, lines, g.cols(slot)]
                copies.append(pltpu.make_async_copy(source, out.at[n, lines], sems.at[n, piece]))
                copies[-1].start()
        mark.wait()
        for n, block in enumerate(blocks):
            for piece in range(PIECES):
                copies[n * PIECES + piece].wait()
            row, slot = g.sent(theirs, block)

            @pl.when(marks[row, slot] == 0)
            def _():
                out[n] = jnp.zeros((width, width), BF16)

    return call(
        kernel,
        [pltpu.HBM, pltpu.HBM],
        [(jax.ShapeDtypeStruct((len(blocks), width, width), BF16), pltpu.VMEM)],
        [
            pltpu.SMEM(mask.shape, jnp.int32),
            pltpu.SemaphoreType.DMA,
            pltpu.SemaphoreType.DMA((len(blocks), PIECES)),
        ],
        (in_hbm(mask), in_hbm(density)),
        name="pack",
    )[0]


def local(g, near_blocks, mask, density):
    rows, width, strip = density.shape
    reach, band = g.reach, g.band

    def kernel(mask_ref, density_ref, out_ref, own, sums, near, gates, done, in_sems, out_sems, near_sems):
        loads = [pltpu.make_async_copy(density_ref.at[r], own.at[r], in_sems.at[r]) for r in range(rows)]
        for load in loads:
            load.start()
        for r in range(rows):
            loads[r].wait()
            for s in range(band):

                @pl.when(mask_ref[r, s] == 0)
                def _():
                    own[r, :, g.cols(s)] = jnp.zeros((width, width), BF16)

                gates[r * band + s] = jnp.full((1, width), mask_ref[r, s].astype(F32))

        stores = []
        for n, block in enumerate(near_blocks):
            row, slot = g.sent(1 - neighbour_side(NEAR), block)
            stores.append(pltpu.make_async_copy(own.at[row, :, g.cols(slot)], near.at[n], near_sems.at[n]))
            stores[-1].start()
        for i in range(rows):
            side = 0 if 2 * i < rows else 1
            final = max(0, band - 2 * reach + g.row(side, i))
            for s in range(band):
                j = i + s - reach
                total = None
                for k in g.inner(i, j, 0, rows - 1):
                    total = add(total, dot(own[i, :, g.cols(k - i + reach)], own[k, :, g.cols(j - k + reach)]))
                ends = s >= band - final if side == 0 else s < final
                if ends:
                    done[i, :, g.cols(s)] = jnp.where(mask_ref[i, s] == 0, 0.0, total).astype(BF16)
                else:
                    sums[i, :, g.cols(s)] = total
            give = g.cols(band - final, final) if side == 0 else g.cols(0, final)
            stores.append(pltpu.make_async_copy(done.at[i, :, give], out_ref.at[i, :, give], out_sems.at[i]))
            stores[-1].start()
        for store in stores:
            store.wait()

    return call(
        kernel,
        [pltpu.SMEM, pltpu.HBM],
        [
            (jax.ShapeDtypeStruct(density.shape, BF16), pltpu.HBM),
            (jax.ShapeDtypeStruct(density.shape, BF16), pltpu.VMEM),
            (jax.ShapeDtypeStruct(density.shape, F32), pltpu.VMEM),
            (jax.ShapeDtypeStruct((len(near_blocks), width, width), BF16), pltpu.VMEM),
            (jax.ShapeDtypeStruct((rows * band, 1, width), F32), pltpu.VMEM),
        ],
        [
            pltpu.VMEM(density.shape, BF16),
            pltpu.SemaphoreType.DMA((rows,)),
            pltpu.SemaphoreType.DMA((rows,)),
            pltpu.SemaphoreType.DMA((len(near_blocks),)),
        ],
        (mask, in_hbm(density)),
        flops=2 * 160 * width**3,
        name="local",
    )


def partials(g, link, own, lists, halos):
    width, reach = g.width, g.reach
    strips = width // LANES
    groups = [g.early_targets, g.final_targets]
    where = {b: (p, n) for p, part in enumerate(lists) for n, b in enumerate(part)}

    def kernel(own_ref, *refs):
        outs = refs[-2:]
        theirs = 1 - neighbour_side(link)
        row_ids = lax.broadcasted_iota(jnp.int32, (CODE_ROWS, LANES), 0)
        powers = jnp.zeros((CODE_ROWS, LANES), F32)
        line = 0
        for out, targets in zip(outs, groups):
            for n, (i, j) in enumerate(targets):
                total = None
                for k in g.inner(i, j, -reach, -1):
                    row, slot = g.sent(theirs, (k, j))
                    p, m = where[-1 - i, -1 - k]
                    total = add(total, dot(refs[p][m], own_ref[row, :, g.cols(slot)]))
                top = jnp.maximum(jnp.max(jnp.abs(total), axis=0, keepdims=True), 2.0**-110)
                power = jnp.ceil(jnp.log2(top) + 0.001)
                code = jnp.round(total * jnp.exp2(CODE_BITS - power)).astype(jnp.int32).astype(jnp.int16)
                for h in range(strips):
                    lanes = slice(h * LANES, (h + 1) * LANES)
                    out[pl.ds((n * strips + h) * width, width), :] = code[:, lanes]
                    powers = jnp.where(row_ids == line, power[:, lanes], powers)
                    line += 1
        outs[0][pl.ds(len(groups[0]) * strips * width, CODE_ROWS), :] = powers.astype(jnp.int32).astype(jnp.int16)

    def result(lines):
        return jax.ShapeDtypeStruct((lines, LANES), jnp.int16), pltpu.VMEM

    return call(
        kernel,
        [pltpu.VMEM] * (1 + len(halos)),
        [result(len(groups[0]) * strips * width + CODE_ROWS), result(len(groups[1]) * strips * width)],
        [],
        (own, *halos),
        flops=WEIGHT * 2 * 8 * width**3,
        name="partials",
    )


def finish(g, link, targets, gates, sums, out, term_of, operands, flops, name):
    width = g.width
    nt, nops = len(targets), len(operands)

    def kernel(gate_ref, sum_ref, *refs):
        ins, (out_ref, done, sems) = refs[:nops], refs[nops + 1 :]
        side = neighbour_side(link)
        stores = []
        for n, (i, j) in enumerate(targets):
            row, slot = g.row(side, i), g.slot(side, i, j)
            value = sum_ref[row, :, g.cols(slot)] + term_of(ins, side, i, j)
            done[n] = (value * gate_ref[row * g.band + slot]).astype(BF16)
            stores.append(pltpu.make_async_copy(done.at[n], out_ref.at[row, :, g.cols(slot)], sems.at[n]))
            stores[-1].start()
        for store in stores:
            store.wait()

    return call(
        kernel,
        [pltpu.VMEM] * (2 + nops) + [pltpu.HBM],
        [(jax.ShapeDtypeStruct(out.shape, out.dtype), pltpu.HBM)],
        [
            pltpu.VMEM((nt, width, width), BF16),
            pltpu.SemaphoreType.DMA((nt,)),
        ],
        (gates, sums, *operands, out),
        aliases={2 + nops: 0},
        flops=flops,
        name=name,
    )[0]


def with_halo(g, link, targets, lists, gates, own, sums, halos, out, name):
    where = {b: (p, n) for p, part in enumerate(lists) for n, b in enumerate(part)}

    def inner(i, j):
        return [k for k in g.inner(i, j, -g.reach, -1) if (k, j) in where]

    def term_of(ins, side, i, j):
        total = None
        for k in inner(i, j):
            p, n = where[k, j]
            total = add(total, dot(ins[0][g.row(side, i), :, g.cols(g.slot(side, i, k))], ins[1 + p][n]))
        return total

    flops = 2 * sum(len(inner(i, j)) for i, j in targets) * g.width**3
    return finish(g, link, targets, gates, sums, out, term_of, (own, *halos), flops, name)


def with_partials(g, link, targets, gates, sums, coded, out, name):
    width = g.width
    strips = width // LANES
    powers_at = len(g.early_targets) * strips * width

    def term_of(ins, side, i, j):
        n, line = targets.index((i, j)), g.last_targets.index((i, j)) * strips
        powers = ins[0][pl.ds(powers_at, CODE_ROWS), :].astype(jnp.int32).astype(F32)
        parts = []
        for h in range(strips):
            code = ins[-1][pl.ds((n * strips + h) * width, width), :].astype(jnp.int32).astype(F32)
            parts.append(code * jnp.exp2(powers[line + h : line + h + 1] - CODE_BITS))
        return jnp.concatenate(parts, axis=1)

    return finish(g, link, targets, gates, sums, out, term_of, coded, 0, name)


def on_device(density, block_mask):
    rows, width, strip = density.shape
    g = Band(rows, width, block_mask.shape[1])
    mask = block_mask
    near_blocks = g.first + g.second + g.rest

    packed_opening = pack(g, FAR, g.opening, mask, density)
    opening = exchange(packed_opening, FAR)
    later, _ = lax.optimization_barrier((mask, packed_opening))
    packed_following = pack(g, FAR, g.following, later, density)
    following = exchange(packed_following, FAR)
    later, _ = lax.optimization_barrier((mask, packed_following))
    packed_second = pack(g, FAR, g.second, later, density)
    second = exchange(packed_second, FAR)
    later, _ = lax.optimization_barrier((mask, packed_second))
    out, own, sums, near, gates = local(g, near_blocks, later, density)
    near = exchange(near, NEAR)

    lists, halos = [g.opening, g.following], [opening, following]
    early, final = partials(g, FAR, own, lists, halos)
    early = exchange(early, FAR)
    final = exchange(final, FAR)
    out = with_halo(g, NEAR, g.targets, [near_blocks], gates, own, sums, [near], out, "near")
    lists, halos = lists + [g.second], halos + [second]
    out = with_halo(g, FAR, g.first_targets + g.second_targets, lists, gates, own, sums, halos, out, "edge")
    out = with_partials(g, FAR, g.early_targets, gates, sums, (early,), out, "early")
    return with_partials(g, FAR, g.final_targets, gates, sums, (early, final), out, "final")


def solution(mesh):
    in_specs = (P(("groups", "grid"), None, None), P(("groups", "grid"), None))
    out_specs = P(("groups", "grid"), None, None)
    return jax.shard_map(on_device, mesh=mesh, in_specs=in_specs, out_specs=out_specs, check_vma=False)
```

```python
import jax
import jax.numpy as jnp
from jax import lax
from jax.experimental import pallas as pl
from jax.experimental.pallas import tpu as pltpu
from jax.sharding import PartitionSpec as P

F32 = jnp.float32
BF16 = jnp.bfloat16
VMEM_BYTES = 26 * 1024 * 1024
CODE_BITS = 15
WEIGHT = 150
CODE_ROWS = 16
LANES = 128
FAR, NEAR = 0, 1


def neighbour_side(link):
    odd = lax.rem(lax.axis_index("grid"), 2)
    return odd if link == FAR else 1 - odd


def exchange(x, link):
    count = lax.axis_size("grid")
    step = [1 if (i % 2 == 0) == (link == NEAR) else -1 for i in range(count)]
    return lax.ppermute(x, "grid", [(i, (i + step[i]) % count) for i in range(count)])


class Band:
    def __init__(self, rows, width, band):
        self.rows = rows
        self.width = width
        self.band = band
        self.reach = reach = (band - 1) // 2
        corner = [(k, j) for k in range(-1, -reach - 1, -1) for j in range(0, k + reach + 1)]
        self.first = [b for b in corner if b[0] > -reach]
        self.opening, self.following = self.first[:2], self.first[2:]
        self.second = [b for b in corner if b[0] == -reach] + [(k, -1) for k in range(-1, -reach - 1, -1)]
        self.rest = [(k, j) for j in range(-2, -reach - 1, -1) for k in range(-1, -reach - 1, -1)]
        self.targets = [(i, j) for i in range(reach) for j in range(i - reach, reach)]
        self.last_targets = [t for t in self.targets if t[1] < -1]
        strips = [(t, h) for t in self.last_targets for h in range(width // LANES)]
        self.returned = [strips[:-2], strips[-2:-1], strips[-1:]]
        self.second_targets = [t for t in self.targets if t[1] == -1 or t == (0, 0)]
        self.first_targets = [t for t in self.targets if t[1] >= 0 and t != (0, 0)]

    def row(self, side, i):
        return i + side * (self.rows - 1 - 2 * i)

    def slot(self, side, i, j):
        return self.reach + (1 - 2 * side) * (j - i)

    def cols(self, slot, count=1):
        start = slot * self.width
        return pl.ds(start if isinstance(start, int) else pl.multiple_of(start, self.width), count * self.width)

    def sent(self, side, block):
        k, j = block
        return (1 - side) * (k + self.rows) + side * (-1 - k), self.slot(side, k, j)

    def inner(self, i, j, low, high):
        return range(max(low, i - self.reach, j - self.reach), min(high, i + self.reach, j + self.reach) + 1)


def dot(a, b):
    return jnp.dot(a, b, preferred_element_type=F32)


def add(total, part):
    return part if total is None else total + part


def spec(space):
    return pl.BlockSpec(memory_space=space)


def in_hbm(x):
    return pltpu.with_memory_space_constraint(x, pltpu.HBM)


def call(kernel, ins, outs, scratch, args, aliases=None, flops=0, name=None):
    moved = sum(a.size * a.dtype.itemsize for a in args) + sum(o.size * o.dtype.itemsize for o, _ in outs)
    return pl.pallas_call(
        kernel,
        out_shape=[o for o, _ in outs],
        in_specs=[spec(space) for space in ins],
        out_specs=[spec(space) for _, space in outs],
        scratch_shapes=scratch,
        input_output_aliases=aliases or {},
        compiler_params=pltpu.CompilerParams(vmem_limit_bytes=VMEM_BYTES),
        cost_estimate=pl.CostEstimate(flops=flops, bytes_accessed=moved, transcendentals=0),
        name=name,
    )(*args)


def pack(g, link, blocks, mask, density):
    width = g.width

    def kernel(mask_ref, density_ref, out, marks, mark_sem, sems):
        theirs = 1 - neighbour_side(link)
        mark = pltpu.make_async_copy(mask_ref, marks, mark_sem)
        mark.start()
        copies = []
        for n, block in enumerate(blocks):
            row, slot = g.sent(theirs, block)
            copies.append(pltpu.make_async_copy(density_ref.at[row, :, g.cols(slot)], out.at[n], sems.at[n]))
            copies[-1].start()
        mark.wait()
        for n, block in enumerate(blocks):
            copies[n].wait()
            row, slot = g.sent(theirs, block)

            @pl.when(marks[row, slot] == 0)
            def _():
                out[n] = jnp.zeros((width, width), BF16)

    return call(
        kernel,
        [pltpu.HBM, pltpu.HBM],
        [(jax.ShapeDtypeStruct((len(blocks), width, width), BF16), pltpu.VMEM)],
        [
            pltpu.SMEM(mask.shape, jnp.int32),
            pltpu.SemaphoreType.DMA,
            pltpu.SemaphoreType.DMA((len(blocks),)),
        ],
        (in_hbm(mask), in_hbm(density)),
        name="pack",
    )[0]


def local(g, near_blocks, mask, density):
    rows, width, strip = density.shape
    reach, band = g.reach, g.band

    def kernel(mask_ref, density_ref, out_ref, own, sums, near, gates, done, in_sems, out_sems, near_sems):
        loads = [pltpu.make_async_copy(density_ref.at[r], own.at[r], in_sems.at[r]) for r in range(rows)]
        for load in loads:
            load.start()
        for r in range(rows):
            loads[r].wait()
            for s in range(band):

                @pl.when(mask_ref[r, s] == 0)
                def _():
                    own[r, :, g.cols(s)] = jnp.zeros((width, width), BF16)

                gates[r * band + s] = jnp.full((1, width), mask_ref[r, s].astype(F32))

        stores = []
        for n, block in enumerate(near_blocks):
            row, slot = g.sent(1 - neighbour_side(NEAR), block)
            stores.append(pltpu.make_async_copy(own.at[row, :, g.cols(slot)], near.at[n], near_sems.at[n]))
            stores[-1].start()
        for i in range(rows):
            side = 0 if 2 * i < rows else 1
            final = max(0, band - 2 * reach + g.row(side, i))
            for s in range(band):
                j = i + s - reach
                total = None
                for k in g.inner(i, j, 0, rows - 1):
                    total = add(total, dot(own[i, :, g.cols(k - i + reach)], own[k, :, g.cols(j - k + reach)]))
                ends = s >= band - final if side == 0 else s < final
                if ends:
                    done[i, :, g.cols(s)] = jnp.where(mask_ref[i, s] == 0, 0.0, total).astype(BF16)
                else:
                    sums[i, :, g.cols(s)] = total
            give = g.cols(band - final, final) if side == 0 else g.cols(0, final)
            stores.append(pltpu.make_async_copy(done.at[i, :, give], out_ref.at[i, :, give], out_sems.at[i]))
            stores[-1].start()
        for store in stores:
            store.wait()

    return call(
        kernel,
        [pltpu.SMEM, pltpu.HBM],
        [
            (jax.ShapeDtypeStruct(density.shape, BF16), pltpu.HBM),
            (jax.ShapeDtypeStruct(density.shape, BF16), pltpu.VMEM),
            (jax.ShapeDtypeStruct(density.shape, F32), pltpu.VMEM),
            (jax.ShapeDtypeStruct((len(near_blocks), width, width), BF16), pltpu.VMEM),
            (jax.ShapeDtypeStruct((rows * band, 1, width), F32), pltpu.VMEM),
        ],
        [
            pltpu.VMEM(density.shape, BF16),
            pltpu.SemaphoreType.DMA((rows,)),
            pltpu.SemaphoreType.DMA((rows,)),
            pltpu.SemaphoreType.DMA((len(near_blocks),)),
        ],
        (mask, in_hbm(density)),
        flops=2 * 160 * width**3,
        name="local",
    )


def partials(g, link, own, lists, halos):
    width, reach = g.width, g.reach
    places = {strip: (m, n) for m, message in enumerate(g.returned) for n, strip in enumerate(message)}
    where = {b: (p, n) for p, part in enumerate(lists) for n, b in enumerate(part)}

    def kernel(own_ref, *refs):
        outs = refs[-len(g.returned) :]
        theirs = 1 - neighbour_side(link)
        row_ids = lax.broadcasted_iota(jnp.int32, (CODE_ROWS, LANES), 0)
        powers = jnp.zeros((CODE_ROWS, LANES), F32)
        line = 0
        for i, j in g.last_targets:
            total = None
            for k in g.inner(i, j, -reach, -1):
                row, slot = g.sent(theirs, (k, j))
                p, m = where[-1 - i, -1 - k]
                total = add(total, dot(refs[p][m], own_ref[row, :, g.cols(slot)]))
            top = jnp.maximum(jnp.max(jnp.abs(total), axis=0, keepdims=True), 2.0**-110)
            power = jnp.ceil(jnp.log2(top) + 0.001)
            code = jnp.round(total * jnp.exp2(CODE_BITS - power)).astype(jnp.int32).astype(jnp.int16)
            for h in range(width // LANES):
                lanes = slice(h * LANES, (h + 1) * LANES)
                m, n = places[(i, j), h]
                outs[m][pl.ds(n * width, width), :] = code[:, lanes]
                powers = jnp.where(row_ids == line, power[:, lanes], powers)
                line += 1
        outs[0][pl.ds(len(g.returned[0]) * width, CODE_ROWS), :] = powers.astype(jnp.int32).astype(jnp.int16)

    lines = [len(message) * width for message in g.returned]
    lines[0] += CODE_ROWS
    return call(
        kernel,
        [pltpu.VMEM] * (1 + len(halos)),
        [(jax.ShapeDtypeStruct((n, LANES), jnp.int16), pltpu.VMEM) for n in lines],
        [],
        (own, *halos),
        flops=WEIGHT * 2 * 8 * width**3,
        name="partials",
    )


def finish(g, link, targets, gates, sums, out, term_of, operands, flops, name):
    width = g.width
    nt, nops = len(targets), len(operands)

    def kernel(gate_ref, sum_ref, *refs):
        ins, (out_ref, done, sems) = refs[:nops], refs[nops + 1 :]
        side = neighbour_side(link)
        stores = []
        for n, (i, j) in enumerate(targets):
            row, slot = g.row(side, i), g.slot(side, i, j)
            value = sum_ref[row, :, g.cols(slot)] + term_of(ins, side, i, j)
            done[n] = (value * gate_ref[row * g.band + slot]).astype(BF16)
            stores.append(pltpu.make_async_copy(done.at[n], out_ref.at[row, :, g.cols(slot)], sems.at[n]))
            stores[-1].start()
        for store in stores:
            store.wait()

    return call(
        kernel,
        [pltpu.VMEM] * (2 + nops) + [pltpu.HBM],
        [(jax.ShapeDtypeStruct(out.shape, out.dtype), pltpu.HBM)],
        [
            pltpu.VMEM((nt, width, width), BF16),
            pltpu.SemaphoreType.DMA((nt,)),
        ],
        (gates, sums, *operands, out),
        aliases={2 + nops: 0},
        flops=flops,
        name=name,
    )[0]


def with_halo(g, link, targets, lists, gates, own, sums, halos, out, name):
    where = {b: (p, n) for p, part in enumerate(lists) for n, b in enumerate(part)}

    def inner(i, j):
        return [k for k in g.inner(i, j, -g.reach, -1) if (k, j) in where]

    def term_of(ins, side, i, j):
        total = None
        for k in inner(i, j):
            p, n = where[k, j]
            total = add(total, dot(ins[0][g.row(side, i), :, g.cols(g.slot(side, i, k))], ins[1 + p][n]))
        return total

    flops = 2 * sum(len(inner(i, j)) for i, j in targets) * g.width**3
    return finish(g, link, targets, gates, sums, out, term_of, (own, *halos), flops, name)


def with_partials(g, link, strips, gates, sums, coded, out, name):
    width = g.width
    order = [strip for message in g.returned for strip in message]
    powers_at = len(g.returned[0]) * width
    ncoded = len(coded)

    def kernel(gate_ref, sum_ref, *refs):
        ins, (out_ref, done, sems) = refs[:ncoded], refs[ncoded + 1 :]
        side = neighbour_side(link)
        powers = ins[0][pl.ds(powers_at, CODE_ROWS), :].astype(jnp.int32).astype(F32)
        stores = []
        for n, ((i, j), h) in enumerate(strips):
            row, slot = g.row(side, i), g.slot(side, i, j)
            cols = pl.ds(pl.multiple_of(slot * width + h * LANES, LANES), LANES)
            line = order.index(((i, j), h))
            code = ins[-1][pl.ds(n * width, width), :].astype(jnp.int32).astype(F32)
            value = sum_ref[row, :, cols] + code * jnp.exp2(powers[line : line + 1] - CODE_BITS)
            done[n] = (value * gate_ref[row * g.band + slot][:, :LANES]).astype(BF16)
            stores.append(pltpu.make_async_copy(done.at[n], out_ref.at[row, :, cols], sems.at[n]))
            stores[-1].start()
        for store in stores:
            store.wait()

    return call(
        kernel,
        [pltpu.VMEM] * (2 + ncoded) + [pltpu.HBM],
        [(jax.ShapeDtypeStruct(out.shape, out.dtype), pltpu.HBM)],
        [
            pltpu.VMEM((len(strips), width, LANES), BF16),
            pltpu.SemaphoreType.DMA((len(strips),)),
        ],
        (gates, sums, *coded, out),
        aliases={2 + ncoded: 0},
        name=name,
    )[0]


def on_device(density, block_mask):
    rows, width, strip = density.shape
    g = Band(rows, width, block_mask.shape[1])
    mask = block_mask
    near_blocks = g.first + g.second + g.rest

    packed_opening = pack(g, FAR, g.opening, mask, density)
    opening = exchange(packed_opening, FAR)
    later, _ = lax.optimization_barrier((mask, packed_opening))
    packed_following = pack(g, FAR, g.following, later, density)
    following = exchange(packed_following, FAR)
    later, _ = lax.optimization_barrier((mask, packed_following))
    packed_second = pack(g, FAR, g.second, later, density)
    second = exchange(packed_second, FAR)
    later, _ = lax.optimization_barrier((mask, packed_second))
    out, own, sums, near, gates = local(g, near_blocks, later, density)
    near = exchange(near, NEAR)

    lists, halos = [g.opening, g.following], [opening, following]
    coded = [exchange(x, FAR) for x in partials(g, FAR, own, lists, halos)]
    out = with_halo(g, NEAR, g.targets, [near_blocks], gates, own, sums, [near], out, "near")
    lists, halos = lists + [g.second], halos + [second]
    out = with_halo(g, FAR, g.first_targets + g.second_targets, lists, gates, own, sums, halos, out, "edge")
    for m, strips in enumerate(g.returned):
        arrived = coded[:1] if m == 0 else [coded[0], coded[m]]
        out = with_partials(g, FAR, strips, gates, sums, arrived, out, "last")
    return out


def solution(mesh):
    in_specs = (P(("groups", "grid"), None, None), P(("groups", "grid"), None))
    out_specs = P(("groups", "grid"), None, None)
    return jax.shard_map(on_device, mesh=mesh, in_specs=in_specs, out_specs=out_specs, check_vma=False)
```
